32 devices in a mesh: section: 2 (over core), dp: 4 (over y, x), tensor: 4 (over z).
Axes of the slice: x: 2, y: 2, z: 4, core: 2. Of those that a mesh axis runs over, the one named last changes fastest.
Arguments:
- edge_in: bfloat16 [2, 2, 2048, 1536], P('section', None, ('dp', 'tensor')), may hold values from -6 to 6
- routes: int32 [2, 2, 2048, 4], P('section', None, 'dp'), may hold values from 0 to 7, all different within a row
- q_weight: bfloat16 [2, 1536, 1536], P('section', 'dp', 'tensor'), may hold values from -0.15625 to 0.15625
- o_weight: bfloat16 [2, 1536, 1536], P('section', 'dp', 'tensor'), may hold values from -3 to 3
- kv_weight: bfloat16 [2, 1536, 512], P('section', ('dp', 'tensor')), may hold values from -0.15625 to 0.15625
- router: bfloat16 [2, 1536, 8], P('section', ('dp', 'tensor')), may hold values from -0.078125 to 0.078125
- gains: bfloat16 [2, 2, 1536], P('section', None, ('dp', 'tensor')), may hold values from 0.5 to 1.5
- w_in: bfloat16 [2, 8, 2, 768, 1536], P('section', 'dp', None, 'tensor'), may hold values from -0.15625 to 0.15625
- w_out: bfloat16 [2, 8, 768, 1536], P('section', 'dp', 'tensor'), may hold values from -0.4375 to 0.4375
Outputs:
- edge_out: float32 [2, 2, 2048, 1536], P('section', None, ('dp', 'tensor'))
- grad_q_weight: float32 [2, 1536, 1536], P('section', 'dp', 'tensor')
- grad_o_weight: float32 [2, 1536, 1536], P('section', 'dp', 'tensor')
- grad_kv_weight: float32 [2, 1536, 512], P('section', ('dp', 'tensor'))
- grad_router: float32 [2, 1536, 8], P('section', ('dp', 'tensor'))
- grad_gains: float32 [2, 2, 1536], P('section', None, ('dp', 'tensor'))
- grad_w_in: float32 [2, 8, 2, 768, 1536], P('section', 'dp', None, 'tensor')
- grad_w_out: float32 [2, 8, 768, 1536], P('section', 'dp', 'tensor')
The draws below stay inside these ranges and needn't reach their ends.
Inputs may be any that keep to these rules, and one draw needn't show every extreme that they name: `routes`: each row names 4 different experts, and every expert is named by some row.
All inputs are finite; a program needn't handle non-finite values.
Results may differ from the reference program's by a relative error of at most 0.03.
Values may be sent and summed in bfloat16 or wider, within the bound.
No kernel may reach another device: no remote copies, remote signals or barrier semaphores. Data moves between devices by JAX's collectives and lax.ppermute only.
A program may use at most 256 MiB of HBM per device.

```python
import math
import jax
import jax.numpy as jnp
from jax import lax

D = 1536
QH = 12
KVH = 2
HD = 128
FF = 768
TOP = 4
MB = 2
PROMPT = 1024
CONT = 256
CONT_DEV = 1
SECTIONS = 2
EXPERTS = 8
PROMPT_DEV = 256
PIECE = 512
TOK = 2048
NCONT = 4
KGROUPS = 4
QGROUP = 3
CAP = 288
N_DP = 4


def level_of(rng, extent, split, smallest, top_value):
    factor_of = 1.0
    for position, blocks in split:
        draws = jax.random.uniform(jax.random.fold_in(jax.random.fold_in(rng, 6), position), (blocks,), jnp.float32, smallest / len(split), top_value / len(split))
        factor_of = factor_of * jnp.repeat(jnp.exp(draws), extent[position] // blocks).reshape((-1,) + (1,) * (len(extent) - 1 - position))
    return factor_of


def picks_of(own_key, rows, count, top, lift):
    ranking = jax.random.permutation(jax.random.fold_in(own_key, 1), count)
    boost = ranking
    for power in range(3):
        boost = boost * boost // count
    boost = boost * lift // count
    tickets = jax.random.randint(jax.random.fold_in(own_key, 2), (rows, count), 0, 4096) + boost
    sure = jax.random.permutation(jax.random.fold_in(own_key, 3), rows)[jnp.arange(count) % rows]
    tickets = jnp.where(jnp.arange(rows)[:, None] == sure[None, :], 1 << 14, tickets)
    priority = tickets * count + jnp.arange(count)
    return lax.top_k(priority.astype(jnp.int32), top)[1].astype(jnp.int32)


def noise(rng, extent, width, limit, split=(), held_as=jnp.bfloat16):
    level = level_of(rng, extent, split, -0.22, 0.18) if split else 1.0
    values = jax.random.normal(rng, extent, jnp.float32) * width * level
    return jnp.minimum(jnp.maximum(values, -limit), limit).astype(held_as)


def setup_inputs(seed: int = 0) -> dict:
    arg_keys = jax.random.split(jax.random.key(seed), 10)
    edge_in = noise(arg_keys[0], (SECTIONS, MB, TOK, D), 1.0, 6.0, ((0, 2), (2, 16)))
    routes = picks_of(arg_keys[1], SECTIONS * MB * TOK, EXPERTS, TOP, 4096).reshape((SECTIONS, MB, TOK, TOP))
    q_weight = noise(arg_keys[2], (SECTIONS, D, QH * HD), D ** -0.5, 0.15625, ((0, 2), (1, 4), (2, 4)))
    o_weight = noise(arg_keys[3], (SECTIONS, D, QH * HD), 4 ** -0.5, 3.0, ((0, 2), (1, 4), (2, 4)))
    kv_weight = noise(arg_keys[4], (SECTIONS, D, 2 * KVH * HD), D ** -0.5, 0.15625, ((0, 2), (1, 16)))
    router = noise(arg_keys[5], (SECTIONS, D, EXPERTS), (4 * D) ** -0.5, 0.078125, ((0, 2), (1, 16)))
    gains = jnp.clip(1.0 + 0.1 * jax.random.normal(arg_keys[6], (SECTIONS, 2, D), jnp.float32), 0.5, 1.5).astype(jnp.bfloat16)
    w_in = noise(arg_keys[7], (SECTIONS, EXPERTS, 2, FF, D), D ** -0.5, 0.15625, ((0, 2), (1, 4), (3, 4)))
    w_out = noise(arg_keys[8], (SECTIONS, EXPERTS, FF, D), (FF // 4) ** -0.5, 0.4375, ((0, 2), (1, 4), (2, 4)))
    return {"edge_in": edge_in, "routes": routes, "q_weight": q_weight, "o_weight": o_weight, "kv_weight": kv_weight, "router": router, "gains": gains, "w_in": w_in, "w_out": w_out}


@jax.custom_vjp
def low(v):
    return lax.optimization_barrier(v.astype(jnp.bfloat16)).astype(jnp.float32)

@jax.custom_vjp
def low_back(v):
    return v

def low_keep(v):
    return (low(v), None)

def low_pass(kept, grad):
    return (grad,)

def back_keep(v):
    return (v, None)

def back_low(kept, grad):
    return (low(grad),)
low.defvjp(low_keep, low_pass)
low_back.defvjp(back_keep, back_low)
EPSILON = 1e-06
NEGATIVE = -1e+30
ROPE_BASE = 10000.0
PRECISE = lax.Precision.HIGHEST

def norm_rows(values, gain):
    return values * lax.rsqrt(lax.optimization_barrier(jnp.mean(values * values, axis=-1, keepdims=True)) + EPSILON) * gain

def rotate(values, places):
    half_width = values.shape[-1] // 2
    frequency = jnp.exp(jnp.arange(half_width, dtype=jnp.float32) * (-math.log(ROPE_BASE) / half_width))
    angles = places.astype(jnp.float32)[:, None] * frequency[None, :]
    angles = angles.reshape((values.shape[0],) + (1,) * (values.ndim - 2) + (half_width,))
    cosine = jnp.cos(angles)
    sine_part = jnp.sin(angles)
    first_half = values[..., :half_width]
    second_half = values[..., half_width:]
    return jnp.concatenate([first_half * cosine - second_half * sine_part, second_half * cosine + first_half * sine_part], axis=-1)

def token_places():
    ordinal = jnp.arange(TOK, dtype=jnp.int32)
    offset = ordinal % PIECE
    return jnp.where(offset < PROMPT_DEV, ordinal // PIECE * PROMPT_DEV + offset, PROMPT + (offset - PROMPT_DEV) % CONT)

def assign_slots(route_ids):
    flat_ids = route_ids.reshape(-1)
    onehot = (flat_ids[:, None] == jnp.arange(EXPERTS, dtype=jnp.int32)[None, :]).astype(jnp.int32)
    before = jnp.cumsum(onehot, axis=0) - onehot
    return lax.optimization_barrier(jnp.sum(before * onehot, axis=1)).reshape(route_ids.shape)

def attend(queries, key_rows, value_rows, allowed):
    scores = low_back(jnp.einsum('hqd,kd->hqk', queries, key_rows, precision=PRECISE) / math.sqrt(HD))
    probability = low(jax.nn.softmax(jnp.where(allowed, scores, NEGATIVE), axis=-1))
    return jnp.einsum('hqk,kd->hqd', probability, value_rows, precision=PRECISE)

def layer_pass(stream, route_ids, q_full, o_full, kv_full, router_full, gain_pair, weight_in, weight_out):
    places = token_places()
    normed = low(norm_rows(stream, gain_pair[0]))
    query_pre = low_back(jnp.dot(normed, q_full, precision=PRECISE))
    key_value = jnp.dot(normed, kv_full, precision=PRECISE)
    queries = low(rotate(query_pre.reshape(TOK, QH, HD), places))
    key_list = []
    value_list = []
    for group_idx in range(KGROUPS):
        kv_head = group_idx * QGROUP // (QH // KVH)
        key_list.append(low(rotate(low_back(key_value[:, kv_head * HD:(kv_head + 1) * HD]), places)))
        value_list.append(low(low_back(key_value[:, (KVH + kv_head) * HD:(KVH + kv_head + 1) * HD])))
    key_rows = jnp.stack(key_list).reshape(KGROUPS, N_DP, PIECE, HD)
    value_rows = jnp.stack(value_list).reshape(KGROUPS, N_DP, PIECE, HD)
    queries = queries.reshape(N_DP, PIECE, KGROUPS, QGROUP, HD).transpose(2, 3, 0, 1, 4)
    prompt_query = queries[:, :, :, :PROMPT_DEV].reshape(KGROUPS, QGROUP, PROMPT, HD)
    cont_query = queries[:, :, :, PROMPT_DEV:].reshape(KGROUPS, QGROUP, NCONT, CONT, HD).transpose(2, 0, 1, 3, 4)
    prompt_keys = key_rows[:, :, :PROMPT_DEV].reshape(KGROUPS, PROMPT, HD)
    prompt_values = value_rows[:, :, :PROMPT_DEV].reshape(KGROUPS, PROMPT, HD)
    cont_keys = key_rows[:, :, PROMPT_DEV:].reshape(KGROUPS, NCONT, CONT, HD).transpose(1, 0, 2, 3)
    cont_values = value_rows[:, :, PROMPT_DEV:].reshape(KGROUPS, NCONT, CONT, HD).transpose(1, 0, 2, 3)
    prompt_ordinal = jnp.arange(PROMPT, dtype=jnp.int32)
    causal = prompt_ordinal[None, :] <= prompt_ordinal[:, None]
    cont_ordinal = jnp.arange(CONT, dtype=jnp.int32)
    cont_allowed = jnp.concatenate([jnp.ones((CONT, PROMPT), jnp.bool_), cont_ordinal[None, :] <= cont_ordinal[:, None]], axis=1)
    prompt_out = lax.map(jax.checkpoint(lambda members: attend(members[0], members[1], members[2], causal)), (prompt_query, prompt_keys, prompt_values))

    def cont_block(members):
        keys_all = jnp.concatenate([prompt_keys, members[1]], axis=1)
        values_all = jnp.concatenate([prompt_values, members[2]], axis=1)
        return jax.vmap(attend, in_axes=(0, 0, 0, None))(members[0], keys_all, values_all, cont_allowed)
    cont_out = lax.map(jax.checkpoint(cont_block), (cont_query, cont_keys, cont_values))
    prompt_out = prompt_out.reshape(KGROUPS, QGROUP, N_DP, PROMPT_DEV, HD)
    cont_out = cont_out.transpose(1, 2, 0, 3, 4).reshape(KGROUPS, QGROUP, N_DP, CONT_DEV * CONT, HD)
    attended = jnp.concatenate([prompt_out, cont_out], axis=3).transpose(2, 3, 0, 1, 4).reshape(TOK, QH * HD)
    attended = low(low_back(attended))
    middle = stream + low_back(jnp.dot(attended, o_full.T, precision=PRECISE))
    moe_in = low(norm_rows(middle, gain_pair[1]))
    logits = low_back(jnp.dot(moe_in, router_full, precision=PRECISE))
    gates = jax.nn.softmax(jnp.take_along_axis(logits, route_ids, axis=1), axis=-1)
    slots = jax.vmap(assign_slots)(route_ids.reshape(N_DP, PIECE, TOP)).reshape(TOK, TOP)
    within = (slots < CAP).astype(jnp.float32)
    piece_of = jnp.broadcast_to((jnp.arange(TOK, dtype=jnp.int32) // PIECE)[:, None], (TOK, TOP))
    spread = jnp.broadcast_to(moe_in[:, None, :], (TOK, TOP, D))
    dispatched = jnp.zeros((N_DP, EXPERTS, CAP + 1, D), jnp.float32).at[piece_of, route_ids, jnp.minimum(slots, CAP)].add(spread)
    dispatched = low_back(dispatched[:, :, :CAP])
    gate_up = low_back(jnp.einsum('pecd,ejfd->pecjf', dispatched, weight_in, precision=PRECISE))
    active = low(jax.nn.gelu(gate_up[..., 0, :]) * gate_up[..., 1, :])
    expert_out = low(low_back(jnp.einsum('pecf,efd->pecd', active, weight_out, precision=PRECISE)))
    picked = expert_out[piece_of, route_ids, jnp.minimum(slots, CAP - 1)]
    return middle + lax.optimization_barrier(jnp.sum((gates * within)[..., None] * picked, axis=1))

def reference(edge_in, routes, q_weight, o_weight, kv_weight, router, gains, w_in, w_out):
    weights = tuple((member.astype(jnp.float32) for member in (q_weight, o_weight, kv_weight, router, gains, w_in, w_out)))
    inputs = edge_in[0].astype(jnp.float32)
    cotangent = edge_in[1].astype(jnp.float32)

    def forward(start, params):
        results = []
        for batch_idx in range(MB):
            hidden = start[batch_idx]
            for section_idx in range(SECTIONS):
                hidden = layer_pass(hidden, routes[section_idx, batch_idx], *[member[section_idx] for member in params])
                if section_idx + 1 < SECTIONS:
                    hidden = low_back(low(hidden))
            results.append(hidden)
        return jnp.stack(results)
    result, pullback = jax.vjp(forward, inputs, weights)
    grad_start, grad_weights = pullback(cotangent)
    return (jnp.stack([grad_start, result]),) + tuple(grad_weights)
```

```python
import math

import jax
import jax.numpy as jnp
from jax import lax
from jax.sharding import PartitionSpec as P

QH = 12
KVH = 2
HD = 128
PROMPT = 1024
CONT = 256

EPSILON = 1e-06
NEGATIVE = -1e30
ROPE_BASE = 10000.0
BF = jnp.bfloat16
F32 = jnp.float32


def dot(left, right, left_axis, right_axis):
    return lax.dot_general(
        left, right, (((left_axis,), (right_axis,)), ((), ())), preferred_element_type=F32
    )


def norm_rows(values, gain):
    return values * lax.rsqrt(jnp.mean(values * values, axis=-1, keepdims=True) + EPSILON) * gain


def gated_act(gate, up):
    return jax.nn.gelu(gate) * up


def section_swap(values):
    return jax.tree.map(lambda v: lax.ppermute(v, "section", [(0, 1), (1, 0)]), values)


def section_send(values, source):
    return jax.tree.map(lambda v: lax.ppermute(v, "section", [(source, 1 - source)]), values)


def dp_swap(values, bit):
    pairs = [(d, d ^ (1 << bit)) for d in range(lax.axis_size("dp"))]
    return lax.ppermute(values, "dp", pairs)


def dp_swap_of(values, bit, section):
    count = lax.axis_size("dp")
    pairs = [(section * count + d, section * count + (d ^ (1 << bit))) for d in range(count)]
    return lax.ppermute(values, ("section", "dp"), pairs)


def dp_bits():
    return lax.axis_size("dp").bit_length() - 1


def slot_source(lane, slot, lanes):
    if slot == 0:
        return lane, None, 0
    if lane < lanes // 2:
        above = lanes - 1 - lane
        if slot <= above:
            return lane + slot, "down", slot
        return lane - (slot - above), "up", slot - above
    if slot <= lane:
        return lane - slot, "up", slot
    return lane + (slot - lane), "down", slot - lane


def slot_origin(slot):
    lanes = lax.axis_size("tensor")
    here = lax.axis_index("tensor")
    origin = jnp.int32(0)
    for lane in range(lanes):
        origin = jnp.where(here == lane, slot_source(lane, slot, lanes)[0], origin)
    return origin


def choose_by_lane(options):
    here = lax.axis_index("tensor")
    groups = []
    for lane, value in enumerate(options):
        if value is None:
            continue
        for group in groups:
            if group[0] is value:
                group[1].append(lane)
                break
        else:
            groups.append((value, [lane]))
    result = groups[0][0]
    for value, where in groups[1:]:
        hit = here == where[0]
        for lane in where[1:]:
            hit = jnp.logical_or(hit, here == lane)
        result = jnp.where(hit, value, result)
    return result


def line_gather(block):
    lanes = lax.axis_size("tensor")
    ups, downs = [block], [block]
    for hop in range(1, lanes):
        ups.append(
            lax.ppermute(ups[-1], "tensor", [(i, i + 1) for i in range(hop - 1, lanes - 1)])
        )
        downs.append(
            lax.ppermute(downs[-1], "tensor", [(i, i - 1) for i in range(1, lanes - hop + 1)])
        )
    slots = [block]
    for slot in range(1, lanes):
        options = []
        for lane in range(lanes):
            _, way, hops = slot_source(lane, slot, lanes)
            options.append(ups[hops] if way == "up" else downs[hops])
        slots.append(choose_by_lane(options))
    return slots


def line_reduce(parts):
    lanes = lax.axis_size("tensor")
    held = parts[0].dtype
    if held == F32:
        total = parts[0]
    else:
        total = parts[0].astype(F32)

    def part_for(lane, origin):
        for slot in range(lanes):
            if slot_source(lane, slot, lanes)[0] == origin:
                return parts[slot]
        return None

    up = down = None
    for step in range(1, lanes):
        away = lanes - step
        up_part = choose_by_lane(
            [part_for(z, z + away) if z + away < lanes else None for z in range(lanes)]
        )
        down_part = choose_by_lane(
            [part_for(z, z - away) if z - away >= 0 else None for z in range(lanes)]
        )
        if up is not None:
            up_part = up_part.astype(F32) + up.astype(F32)
            down_part = down_part.astype(F32) + down.astype(F32)
        up = lax.ppermute(
            up_part.astype(BF), "tensor", [(i, i + 1) for i in range(step) if i + 1 < lanes]
        )
        down = lax.ppermute(
            down_part.astype(BF), "tensor", [(i, i - 1) for i in range(away, lanes) if i >= 1]
        )
    return total + up.astype(F32) + down.astype(F32)


def cube_gather(block, bits):
    for bit in bits:
        block = jnp.concatenate([block, dp_swap(block, bit)], axis=0)
    return block


def cube_reduce(parts, bits):
    for bit in reversed(bits):
        half = parts.shape[0] // 2
        arrived = dp_swap(parts[half:].astype(BF), bit)
        parts = parts[:half].astype(F32) + arrived.astype(F32)
    return parts


def rows_gather(block):
    bits = range(1, dp_bits())
    return [cube_gather(slot[None], bits) for slot in line_gather(block)]


def rows_reduce(parts):
    bits = range(1, dp_bits())
    reduced = [None] * len(parts)
    for slot in reversed(range(len(parts))):
        reduced[slot] = cube_reduce(parts[slot], bits)[0]
    return line_reduce(reduced)


def rope_tables(places):
    half = HD // 2
    frequency = jnp.exp(jnp.arange(half, dtype=F32) * (-math.log(ROPE_BASE) / half))
    angles = places.astype(F32)[:, None] * frequency[None, :]
    return jnp.cos(angles), jnp.sin(angles)


def rotate(values, tables, sign):
    cosine, sine = tables[0][:, None, :], sign * tables[1][:, None, :]
    half = HD // 2
    first, second = values[..., :half], values[..., half:]
    return jnp.concatenate(
        [first * cosine - second * sine, second * cosine + first * sine], axis=-1
    )


def key_value_gather(key_value, prompt_dev):
    rows, width = key_value.shape
    lanes = lax.axis_size("tensor")
    piece = jnp.zeros((rows * lanes, width), key_value.dtype)
    for slot, block in enumerate(line_gather(key_value)):
        piece = lax.dynamic_update_slice_in_dim(piece, block, slot_origin(slot) * rows, 0)
    prompt = cube_gather(piece[None, :prompt_dev], range(dp_bits()))
    return jnp.concatenate([prompt.reshape(-1, width), piece[prompt_dev:]], axis=0)


def key_value_reduce(grads, prompt_dev, rows):
    width = grads.shape[1]
    pieces = lax.axis_size("dp")
    prompt = cube_reduce(grads[:PROMPT].reshape(pieces, prompt_dev, width), range(dp_bits()))
    piece = jnp.concatenate([prompt[0], grads[PROMPT:]], axis=0)
    lanes = lax.axis_size("tensor")
    return line_reduce(
        [
            lax.dynamic_slice_in_dim(piece, slot_origin(slot) * rows, rows, 0)
            for slot in range(lanes)
        ]
    )


def allowed_pairs(rows, piece_rows, prompt_dev):
    piece_index = lax.axis_index("dp")
    ordinal = lax.axis_index("tensor") * rows + jnp.arange(rows, dtype=jnp.int32)
    columns = jnp.arange(PROMPT + piece_rows - prompt_dev, dtype=jnp.int32)
    key_place = (jnp.bitwise_xor(columns // prompt_dev, piece_index)) * prompt_dev + (
        columns % prompt_dev
    )
    query_prompt = ordinal < prompt_dev
    query_place = piece_index * prompt_dev + ordinal
    query_cont = (ordinal - prompt_dev) // CONT
    query_step = (ordinal - prompt_dev) % CONT
    local_col = columns - PROMPT
    prompt_part = jnp.logical_or(
        jnp.logical_not(query_prompt)[:, None], key_place[None, :] <= query_place[:, None]
    )
    cont_part = jnp.logical_and(
        jnp.logical_not(query_prompt)[:, None],
        jnp.logical_and(
            local_col[None, :] // CONT == query_cont[:, None],
            local_col[None, :] % CONT <= query_step[:, None],
        ),
    )
    return jnp.where((columns < PROMPT)[None, :], prompt_part, cont_part)


def own_places(rows, prompt_dev):
    piece_index = lax.axis_index("dp")
    ordinal = lax.axis_index("tensor") * rows + jnp.arange(rows, dtype=jnp.int32)
    return jnp.where(
        ordinal < prompt_dev,
        piece_index * prompt_dev + ordinal,
        PROMPT + (ordinal - prompt_dev) % CONT,
    )


def by_head(values, heads):
    rows = values.shape[0]
    return values.reshape(rows, heads, HD).transpose(1, 0, 2).reshape(KVH, -1, HD)


def from_heads(values, heads):
    rows = values.shape[0] * values.shape[1] // heads
    return values.reshape(heads, rows, HD).transpose(1, 0, 2).reshape(rows, heads * HD)


def batched(left, right, left_axis, right_axis):
    return lax.dot_general(
        left, right, (((left_axis,), (right_axis,)), ((0,), (0,))), preferred_element_type=F32
    )


def attention_forward(stream, weights, plan):
    rows = stream.shape[0]
    normed = norm_rows(stream, weights["gains"][0]).astype(BF)
    query_pre = dot(normed, weights["q"], 1, 0)
    key_value = dot(normed, weights["kv"], 1, 0)
    queries = rotate(query_pre.reshape(rows, QH, HD), plan["rope"], 1.0).astype(BF)
    queries = queries.transpose(1, 0, 2).reshape(KVH, -1, HD)
    keys = rotate(key_value[:, : KVH * HD].reshape(rows, KVH, HD), plan["rope"], 1.0)
    packed = jnp.concatenate(
        [keys.reshape(rows, KVH * HD), key_value[:, KVH * HD :]], axis=1
    ).astype(BF)
    seen = key_value_gather(packed, plan["prompt_dev"])
    key_rows = seen[:, : KVH * HD].reshape(-1, KVH, HD).transpose(1, 0, 2)
    value_rows = seen[:, KVH * HD :].reshape(-1, KVH, HD).transpose(1, 0, 2)
    scores = batched(queries, key_rows, 2, 2) * (1.0 / math.sqrt(HD))
    shape = scores.shape
    scores = scores.reshape(KVH, -1, rows, shape[-1])
    scores = jnp.where(plan["allowed"], scores, NEGATIVE)
    highest = jnp.max(scores, axis=-1, keepdims=True)
    exponent = jnp.exp(scores - highest)
    probability = exponent / jnp.sum(exponent, axis=-1, keepdims=True)
    probability = probability.reshape(shape)
    attended = from_heads(batched(probability.astype(BF), value_rows, 2, 1), QH).astype(BF)
    middle = stream + dot(attended, weights["o"], 1, 1)
    return middle, (normed, queries, key_rows, value_rows, probability, attended)


def attention_backward(grad_middle, stream, kept, weights, plan):
    normed, queries, key_rows, value_rows, probability, attended = kept
    rows = stream.shape[0]
    scale = 1.0 / math.sqrt(HD)
    grad_branch = grad_middle.astype(BF)
    grad_o = dot(grad_branch, attended, 0, 0)
    grad_attended = by_head(dot(grad_branch, weights["o"], 1, 0).astype(BF), QH)
    grad_prob = batched(grad_attended, value_rows, 2, 2)
    delta = jnp.sum(probability * grad_prob, axis=-1, keepdims=True)
    grad_scores = (probability * (grad_prob - delta)).astype(BF)
    grad_query = batched(grad_scores, key_rows, 2, 1) * scale
    grad_keys = batched(grad_scores, queries, 1, 1) * scale
    grad_values = batched(probability.astype(BF), grad_attended, 1, 1)
    grads = jnp.concatenate([grad_keys, grad_values], axis=0)
    grads = grads.transpose(1, 0, 2).reshape(-1, 2 * KVH * HD)
    grads = key_value_reduce(grads, plan["prompt_dev"], rows)
    grad_keys = rotate(grads[:, : KVH * HD].reshape(rows, KVH, HD), plan["rope"], -1.0)
    grad_kv = jnp.concatenate(
        [grad_keys.reshape(rows, KVH * HD), grads[:, KVH * HD :]], axis=1
    ).astype(BF)
    grad_query = grad_query.reshape(QH, rows, HD).transpose(1, 0, 2)
    grad_query_pre = rotate(grad_query, plan["rope"], -1.0).reshape(rows, QH * HD).astype(BF)
    grad_normed = dot(grad_query_pre, weights["q"], 1, 1) + dot(grad_kv, weights["kv"], 1, 1)
    grad_q = dot(normed, grad_query_pre, 0, 0)
    grad_kv_weight = dot(normed, grad_kv, 0, 0)
    _, pull = jax.vjp(norm_rows, stream, weights["gains"][0])
    grad_stream, grad_gain = pull(grad_normed)
    return grad_stream + grad_middle, grad_q, grad_o, grad_kv_weight, grad_gain


def route_masks(route_ids, experts, capacity):
    ids = jnp.arange(experts, dtype=jnp.int32)
    chosen = jnp.sum((route_ids[:, :, None] == ids[None, None, :]).astype(F32), axis=1)
    rows = route_ids.shape[0]
    ordinal = jnp.arange(rows, dtype=jnp.int32)
    before = (ordinal[:, None] > ordinal[None, :]).astype(BF)
    slots = dot(before, chosen.astype(BF), 1, 0)
    kept = jnp.where(slots < capacity, chosen, 0.0)
    return chosen.astype(BF), kept.astype(BF)


def gate_values(logits, chosen):
    masked = jnp.where(chosen > 0, logits, NEGATIVE)
    exponent = jnp.exp(masked - jnp.max(masked, axis=-1, keepdims=True))
    return exponent / jnp.sum(exponent, axis=-1, keepdims=True)


def experts_forward(middle, weights, masks, plan):
    moe_in = norm_rows(middle, weights["gains"][1]).astype(BF)
    width = moe_in.shape[1]
    parts, kept = [], []
    for slot, block in enumerate(rows_gather(moe_in)):
        groups, rows = block.shape[0], block.shape[1]
        block = block.reshape(groups * rows, width)
        chosen, within = masks[slot]
        gates = gate_values(dot(block, weights["router"], 1, 0), chosen) * within
        spread = lax.dot_general(
            gates,
            plan["spread"],
            (((1,), (0,)), ((), ())),
            precision=lax.Precision.HIGHEST,
            preferred_element_type=F32,
        )
        gate = dot(block, weights["gate"], 1, 1)
        up = dot(block, weights["up"], 1, 1)
        weighted = (gated_act(gate, up) * spread).astype(BF)
        out = dot(weighted, weights["down"], 1, 0)
        parts.append(out.reshape(groups, rows, width))
        kept.append((block, gate, up, spread, weighted))
    return moe_in, parts, kept


def experts_backward(grad_blocks, kept, weights, plan):
    joined = [jnp.concatenate(members, axis=0) for members in zip(*kept)]
    block, gate, up, spread, weighted = joined
    groups, rows, width = grad_blocks[0].shape
    grad = jnp.concatenate([g.reshape(-1, width) for g in grad_blocks], axis=0)
    grad_raw = dot(grad, weights["down"], 1, 1)
    active, pull = jax.vjp(gated_act, gate, up)
    gate_terms = (grad_raw * active).astype(BF)
    grad_gates = dot(plan["spread"].astype(BF), gate_terms, 1, 1)
    grad_gate, grad_up = pull(grad_raw * spread)
    grad_gate, grad_up = grad_gate.astype(BF), grad_up.astype(BF)
    grad_block = dot(grad_gate, weights["gate"], 1, 0) + dot(grad_up, weights["up"], 1, 0)
    experts = grad_gates.shape[0]
    slots = len(grad_blocks)
    grad_block = grad_block.reshape(slots, groups, rows, width)
    grad_gates = grad_gates.reshape(experts, slots, groups, rows).transpose(1, 2, 0, 3)
    grads = (
        dot(grad_gate, block, 0, 0),
        dot(grad_up, block, 0, 0),
        dot(weighted, grad, 0, 0),
    )
    return (
        [grad_block[slot] for slot in range(slots)],
        [grad_gates[slot] for slot in range(slots)],
        grads,
    )


def layer_backward(grad_out, grad_blocks, kept, weights, plan):
    stream, attention_kept, middle, moe_in, experts_kept, chosen, within = kept
    parts, gate_parts, expert_grads = experts_backward(grad_blocks, experts_kept, weights, plan)
    grad_moe = rows_reduce(parts)
    grad_gate = rows_reduce(gate_parts).T * within
    gates = gate_values(dot(moe_in, weights["router"], 1, 0), chosen)
    grad_logits = gates * (grad_gate - jnp.sum(gates * grad_gate, axis=-1, keepdims=True))
    grad_logits = grad_logits.astype(BF)
    grad_moe = grad_moe + dot(grad_logits, weights["router"], 1, 1)
    grad_router = dot(moe_in, grad_logits, 0, 0)
    _, pull = jax.vjp(norm_rows, middle, weights["gains"][1])
    grad_middle, grad_gain_moe = pull(grad_moe)
    grad_middle = grad_middle + grad_out
    grad_stream, grad_q, grad_o, grad_kv, grad_gain = attention_backward(
        grad_middle, stream, attention_kept, weights, plan
    )
    small = (grad_kv, grad_router, jnp.stack([grad_gain, grad_gain_moe]))
    return grad_stream, (grad_q, grad_o, small, expert_grads)


def two_layers(own):
    leading = lax.axis_index("section") == 0
    other = section_swap(own)
    first = jax.tree.map(lambda a, b: jnp.where(leading, a, b), own, other)
    second = jax.tree.map(lambda a, b: jnp.where(leading, b, a), own, other)
    return first, second


def pair_experts(own, layer):
    partner = dp_swap_of(own, 0, layer)
    there = section_send((own, partner), layer)
    here = lax.axis_index("section") == layer
    both = [jnp.where(here, a, b) for a, b in zip((own, partner), there)]
    return [jnp.concatenate([both[0][j], both[1][j]], axis=0) for j in range(3)]


def spread_matrix(experts, local, units):
    piece_index = lax.axis_index("dp")
    column = jnp.arange(2 * local * units, dtype=jnp.int32)
    owner = jnp.bitwise_xor(piece_index, column // (local * units))
    expert = owner * local + column % (local * units) // units
    return (jnp.arange(experts, dtype=jnp.int32)[:, None] == expert[None, :]).astype(F32)


def per_device(edge_in, routes, q_weight, o_weight, kv_weight, router, gains, w_in, w_out):
    section = lax.axis_index("section")
    leading = section == 0
    lanes = lax.axis_size("tensor")
    pieces = lax.axis_size("dp")
    rows = edge_in.shape[2]
    piece_rows = rows * lanes
    prompt_dev = PROMPT // pieces
    local, units, width = w_out.shape[1:]
    experts = local * pieces
    top = routes.shape[3]
    capacity = lanes * (
        (9 * piece_rows * top + 8 * experts * lanes - 1) // (8 * experts * lanes)
    )

    edge_kept = lax.dynamic_index_in_dim(edge_in[0], section, 0, keepdims=False)
    edge_got = section_swap(lax.dynamic_index_in_dim(edge_in[0], 1 - section, 0, keepdims=False))
    stream = jnp.where(leading, edge_kept, edge_got).astype(F32)
    cotangent = jnp.where(leading, edge_got, edge_kept)
    route_kept = lax.dynamic_index_in_dim(routes[0], section, 0, keepdims=False)
    route_got = section_swap(lax.dynamic_index_in_dim(routes[0], 1 - section, 0, keepdims=False))
    route_first = jnp.where(leading, route_kept, route_got)
    route_second = jnp.where(leading, route_got, route_kept)

    q_own = lax.all_gather(lax.all_gather(q_weight[0], "dp", axis=0, tiled=True), "tensor", axis=1, tiled=True)
    o_own = lax.all_gather(lax.all_gather(o_weight[0], "dp", axis=0, tiled=True), "tensor", axis=1, tiled=True)
    small = jnp.concatenate([kv_weight[0], router[0], gains[0].T], axis=1)
    small_own = lax.all_gather(small, ("dp", "tensor"), axis=0, tiled=True)
    layers = two_layers((q_own, o_own, small_own))
    expert_own = jnp.stack(
        [
            w_in[0, :, 0].reshape(local * units, width),
            w_in[0, :, 1].reshape(local * units, width),
            w_out[0].reshape(local * units, width),
        ]
    )
    weights = []
    kv_cols = kv_weight.shape[2]
    for layer in range(2):
        q_full, o_full, small_full = layers[layer]
        gate, up, down = pair_experts(expert_own, layer)
        weights.append(
            {
                "q": q_full,
                "o": o_full,
                "kv": small_full[:, :kv_cols],
                "router": small_full[:, kv_cols : kv_cols + experts],
                "gains": small_full[:, kv_cols + experts :].T.astype(F32),
                "gate": gate,
                "up": up,
                "down": down,
            }
        )

    plan = {
        "prompt_dev": prompt_dev,
        "rope": rope_tables(own_places(rows, prompt_dev)),
        "allowed": allowed_pairs(rows, piece_rows, prompt_dev),
        "spread": spread_matrix(experts, local, units),
    }
    own_masks = [route_masks(ids, experts, capacity) for ids in (route_first, route_second)]
    all_masks = cube_gather(
        jnp.concatenate([m for pair in own_masks for m in pair], axis=1)[None],
        range(1, dp_bits()),
    )
    origins = [slot_origin(slot) for slot in range(lanes)]
    masks = ([], [])
    for slot in range(lanes):
        piece = lax.dynamic_slice_in_dim(all_masks, origins[slot] * rows, rows, 1)
        piece = piece.reshape(-1, 4 * experts).astype(F32)
        for layer in range(2):
            first = 2 * layer * experts
            masks[layer].append(
                (piece[:, first : first + experts], piece[:, first + experts : first + 2 * experts])
            )

    saved = []
    hidden = stream
    for layer in range(2):
        middle, attention_kept = attention_forward(hidden, weights[layer], plan)
        moe_in, parts, experts_kept = experts_forward(
            middle, weights[layer], masks[layer], plan
        )
        result = middle + rows_reduce(parts)
        chosen, within = (member[:rows] for member in masks[layer][0])
        saved.append((hidden, attention_kept, middle, moe_in, experts_kept, chosen, within))
        if layer == 0:
            hidden = result.astype(BF).astype(F32)

    grad_out = cotangent
    grads = [None, None]
    for layer in (1, 0):
        grad_blocks = rows_gather(grad_out)
        grad_stream, grads[layer] = layer_backward(
            grad_out.astype(F32), grad_blocks, saved[layer], weights[layer], plan
        )
        grad_out = grad_stream.astype(BF)

    edge_kept = jnp.where(leading, grad_stream, result)
    edge_got = section_swap(jnp.where(leading, result, grad_stream))
    edge_out = jnp.where(
        leading, jnp.stack([edge_kept, edge_got]), jnp.stack([edge_got, edge_kept])
    )

    def own_layer(first, second):
        keep = jax.tree.map(lambda a, b: jnp.where(leading, a, b), first, second)
        send = jax.tree.map(lambda a, b: jnp.where(leading, b, a).astype(BF), first, second)
        return jax.tree.map(lambda a, b: a + b.astype(F32), keep, section_swap(send))

    grad_q, grad_o, grad_small, grad_experts = own_layer(grads[0], grads[1])

    def square(total):
        total = lax.psum_scatter(total.astype(BF), "dp", scatter_dimension=0, tiled=True)
        return lax.psum_scatter(total, "tensor", scatter_dimension=1, tiled=True).astype(F32)

    grad_small = jnp.concatenate([grad_small[0], grad_small[1], grad_small[2].T], axis=1)
    grad_small = lax.psum_scatter(
        grad_small, ("dp", "tensor"), scatter_dimension=0, tiled=True
    )
    owned = local * units
    partner = [lax.ppermute(
        member[owned:].astype(BF), "dp", [(d, d ^ 1) for d in range(pieces)]
    ) for member in grad_experts]
    grad_gate, grad_up, grad_down = [
        (member[:owned] + got.astype(F32)).reshape(local, units, width)
        for member, got in zip(grad_experts, partner)
    ]
    return (
        edge_out[None],
        square(grad_q)[None],
        square(grad_o)[None],
        grad_small[None, :, :kv_cols],
        grad_small[None, :, kv_cols : kv_cols + experts],
        grad_small[:, kv_cols + experts :].T[None],
        jnp.stack([grad_gate, grad_up], axis=1)[None],
        grad_down[None],
    )


def solution(mesh):
    placed = (
        P("section", None, ("dp", "tensor"), None),
        P("section", None, "dp", None),
        P("section", "dp", "tensor"),
        P("section", "dp", "tensor"),
        P("section", ("dp", "tensor"), None),
        P("section", ("dp", "tensor"), None),
        P("section", None, ("dp", "tensor")),
        P("section", "dp", None, "tensor", None),
        P("section", "dp", "tensor", None),
    )
    return jax.shard_map(
        per_device,
        mesh=mesh,
        in_specs=placed,
        out_specs=(placed[0],) + placed[2:],
        check_vma=False,
    )
```

```python
import math

import jax
import jax.numpy as jnp
from jax import lax
from jax.experimental import pallas as pl
from jax.experimental.pallas import tpu as pltpu
from jax.sharding import PartitionSpec as P

QH = 12
KVH = 2
HD = 128
PROMPT = 1024
CONT = 256

EPSILON = 1e-06
NEGATIVE = -1e30
ROPE_BASE = 10000.0
BF = jnp.bfloat16
F32 = jnp.float32
VMEM_BYTES = 56 * 1024 * 1024
GELU_SCALE = math.sqrt(2.0 / math.pi)
GELU_CUBE = 0.044715


def dot(left, right, left_axis, right_axis):
    return lax.dot_general(
        left, right, (((left_axis,), (right_axis,)), ((), ())), preferred_element_type=F32
    )


def norm_rows(values, gain):
    return values * lax.rsqrt(jnp.mean(values * values, axis=-1, keepdims=True) + EPSILON) * gain


def gelu_parts(values):
    square = values * values
    bent = jnp.tanh(GELU_SCALE * values * (1.0 + GELU_CUBE * square))
    half = 0.5 * (1.0 + bent)
    slope = half + 0.5 * values * (1.0 - bent * bent) * (
        GELU_SCALE * (1.0 + 3.0 * GELU_CUBE * square)
    )
    return values * half, slope


def kernel_params(axes):
    return pltpu.CompilerParams(
        vmem_limit_bytes=VMEM_BYTES, dimension_semantics=("arbitrary",) * axes
    )


def tree_swap(values, axis, pairs):
    return jax.tree.map(lambda v: lax.ppermute(v, axis, pairs), values)


def section_swap(values):
    return tree_swap(values, "section", [(0, 1), (1, 0)])


def section_send(values, source):
    return tree_swap(values, "section", [(source, 1 - source)])


def dp_bits():
    return lax.axis_size("dp").bit_length() - 1


def stage_bit(section, stage):
    return stage if section == 0 else dp_bits() - 1 - stage


def stage_swap(values, stage):
    count = lax.axis_size("dp")
    pairs = [
        (s * count + d, s * count + (d ^ (1 << stage_bit(s, stage))))
        for s in range(2)
        for d in range(count)
    ]
    return lax.ppermute(values, ("section", "dp"), pairs)


def stage_origin(position):
    origins = []
    for section in range(2):
        moved = jnp.int32(0)
        for stage in range(dp_bits()):
            moved = moved | ((position >> stage) & 1) << stage_bit(section, stage)
        origins.append(moved)
    return lax.axis_index("dp") ^ jnp.where(lax.axis_index("section") == 0, *origins)


def stage_position(origin):
    moved = origin ^ lax.axis_index("dp")
    positions = []
    for section in range(2):
        position = jnp.int32(0)
        for stage in range(dp_bits()):
            position = position | ((moved >> stage_bit(section, stage)) & 1) << stage
        positions.append(position)
    return jnp.where(lax.axis_index("section") == 0, *positions)


def stage_join(block, stage, until):
    moved = stage_swap(block, stage)
    if until is not None:
        moved = tie(moved, until)
    return jnp.concatenate([block, moved], axis=0)


def staged_gather(block, until=()):
    block = block[None]
    for stage in range(dp_bits()):
        block = stage_join(block, stage, until[min(stage, len(until) - 1)] if until else None)
    return block


def staged_reduce(parts):
    for stage in reversed(range(dp_bits())):
        half = parts.shape[0] // 2
        arrived = stage_swap(parts[half:].astype(BF), stage)
        parts = parts[:half].astype(F32) + arrived.astype(F32)
    return parts[0].astype(F32)


def to_staged(values):
    pieces = lax.axis_size("dp")
    size = values.shape[1] // pieces
    return jnp.concatenate(
        [
            lax.dynamic_slice_in_dim(values, stage_origin(p) * size, size, 1)
            for p in range(pieces)
        ],
        axis=1,
    )


def from_staged(values, axis=1):
    pieces = lax.axis_size("dp")
    size = values.shape[axis] // pieces
    return jnp.concatenate(
        [
            lax.dynamic_slice_in_dim(values, stage_position(jnp.int32(d)) * size, size, axis)
            for d in range(pieces)
        ],
        axis=axis,
    )


def mirrored():
    here = lax.axis_index("tensor")
    return jnp.where(lax.axis_index("section") == 0, here, lax.axis_size("tensor") - 1 - here)


def mirrored_send(values, pairs):
    lanes = lax.axis_size("tensor")
    routes = [(a, b) for a, b in pairs]
    routes += [(2 * lanes - 1 - a, 2 * lanes - 1 - b) for a, b in pairs]
    return lax.ppermute(values, ("section", "tensor"), routes)


def holders_gather(block, until=None):
    place = mirrored()
    near = mirrored_send(block, [(0, 1), (1, 2)])
    far = mirrored_send(block, [(0, 2), (1, 3)])
    last = mirrored_send(block, [(0, 3), (1, 0)])
    if until is not None:
        near, far, last = tie((near, far, last), until)
    outer = jnp.where(
        place == 0, block, jnp.where(place == 1, near, jnp.where(place == 2, far, last))
    )
    inner = jnp.where(
        place == 0, last, jnp.where(place == 1, block, jnp.where(place == 2, near, far))
    )
    leading = lax.axis_index("section") == 0
    return jnp.concatenate(
        [jnp.where(leading, outer, inner), jnp.where(leading, inner, outer)], axis=1
    )


def holders_reduce(parts):
    place = mirrored()
    leading = lax.axis_index("section") == 0
    cols = parts.shape[1] // 2
    outer = jnp.where(leading, parts[:, :cols], parts[:, cols:])
    inner = jnp.where(leading, parts[:, cols:], parts[:, :cols])
    total = jnp.where(place == 0, outer, inner)
    outer, inner = outer.astype(BF), inner.astype(BF)
    near = mirrored_send(jnp.where(place == 1, outer, inner), [(1, 0), (2, 1)])
    far = mirrored_send(jnp.where(place == 2, outer, inner), [(2, 0), (3, 1)])
    last = mirrored_send(jnp.where(place == 3, outer, inner), [(3, 0), (0, 1)])
    return total + near.astype(F32) + far.astype(F32) + last.astype(F32)


def lanes_gather(block, axis):
    lanes = lax.axis_size("tensor")
    here = lax.axis_index("tensor")
    blocks = [block]
    for apart in range(1, lanes):
        blocks.append(
            lax.ppermute(block, "tensor", [(i, (i - apart) % lanes) for i in range(lanes)])
        )
    size = block.shape[axis]
    return lax.dynamic_slice_in_dim(
        jnp.concatenate(blocks + blocks[: lanes - 1], axis=axis),
        jnp.where(here == 0, 0, lanes - here) * size,
        lanes * size,
        axis,
    )


def lanes_reduce(parts):
    lanes = lax.axis_size("tensor")
    here = lax.axis_index("tensor")
    total = lax.dynamic_index_in_dim(parts, here, 0, keepdims=False)
    for apart in range(1, lanes):
        term = lax.dynamic_index_in_dim(parts, (here + apart) % lanes, 0, keepdims=False)
        pairs = [(i, (i + apart) % lanes) for i in range(lanes)]
        total = total + lax.ppermute(term.astype(BF), "tensor", pairs).astype(F32)
    return total


def tie(values, event):
    probe = event[(0,) * event.ndim]
    return jax.tree.map(lambda v: jnp.where(probe != probe, jnp.zeros((), v.dtype), v), values)


def rows_gather(block):
    mine = staged_gather(block).reshape(-1, block.shape[1])
    return mine, section_swap(mine)


def rows_reduce(mine, other, rows):
    total = mine + section_swap(other.astype(BF)).astype(F32)
    return staged_reduce(total.reshape(-1, rows, total.shape[1]))


def rope_tables(places):
    half = HD // 2
    frequency = jnp.exp(jnp.arange(half, dtype=F32) * (-math.log(ROPE_BASE) / half))
    angles = places.astype(F32)[:, None] * frequency[None, :]
    cosine, sine = jnp.cos(angles), jnp.sin(angles)
    return (
        jnp.concatenate([cosine, cosine], axis=1),
        jnp.concatenate([-sine, sine], axis=1),
    )


def rotate(values, tables, sign):
    half = HD // 2
    turned = jnp.concatenate([values[:, half:], values[:, :half]], axis=1)
    return values * tables[0] + turned * (sign * tables[1])


def key_value_gather(key_value, prompt_dev):
    piece = lanes_gather(key_value, 1)
    return staged_gather(piece[:, :prompt_dev]), piece


def lanes_parts(piece, rows):
    batches, _, width = piece.shape
    return piece.reshape(batches, -1, rows, width).transpose(1, 0, 2, 3)


def allowed_pairs(rows, piece_rows, prompt_dev):
    piece_index = lax.axis_index("dp")
    ordinal = lax.axis_index("tensor") * rows + jnp.arange(rows, dtype=jnp.int32)
    columns = jnp.arange(PROMPT + piece_rows - prompt_dev, dtype=jnp.int32)
    key_place = stage_origin(columns // prompt_dev) * prompt_dev + columns % prompt_dev
    query_prompt = ordinal < prompt_dev
    query_place = piece_index * prompt_dev + ordinal
    query_cont = (ordinal - prompt_dev) // CONT
    query_step = (ordinal - prompt_dev) % CONT
    local_col = columns - PROMPT
    prompt_part = jnp.logical_or(
        jnp.logical_not(query_prompt)[:, None], key_place[None, :] <= query_place[:, None]
    )
    cont_part = jnp.logical_and(
        jnp.logical_not(query_prompt)[:, None],
        jnp.logical_and(
            local_col[None, :] // CONT == query_cont[:, None],
            local_col[None, :] % CONT <= query_step[:, None],
        ),
    )
    return jnp.where((columns < PROMPT)[None, :], prompt_part, cont_part)


def own_places(rows, prompt_dev):
    piece_index = lax.axis_index("dp")
    ordinal = lax.axis_index("tensor") * rows + jnp.arange(rows, dtype=jnp.int32)
    return jnp.where(
        ordinal < prompt_dev,
        piece_index * prompt_dev + ordinal,
        PROMPT + (ordinal - prompt_dev) % CONT,
    )


def with_other(values):
    return jnp.concatenate([values, section_swap(values)], axis=0)


def sum_with_other(values):
    rows = values.shape[0] // 2
    return values[:rows] + section_swap(values[rows:].astype(BF)).astype(F32)


def attend_kernel(query_ref, prompt_ref, piece_ref, bias_ref, cos_ref, sin_ref, *refs):
    out_ref, queries_ref, rows_ref, scores_ref, probs_ref = refs[-5:]
    rows, cols = query_ref.shape
    heads = cols // HD
    prompt_dev = prompt_ref.shape[2]
    seen = rows_ref.shape[0]
    rows_ref[:PROMPT] = prompt_ref[...].reshape(PROMPT, 2 * HD)
    rows_ref[PROMPT:] = piece_ref[0, prompt_dev:]
    cosine, sine = cos_ref[...], sin_ref[...]
    queries = []
    for head in range(heads):
        part = query_ref[:, head * HD : (head + 1) * HD]
        part = part * cosine + pltpu.roll(part, HD // 2, 1) * sine
        part = part.astype(BF)
        queries_ref[:, head * HD : (head + 1) * HD] = part
        queries.append(part)
    keys, values = rows_ref[:, :HD], rows_ref[:, HD:]
    scores_ref[...] = dot(jnp.concatenate(queries, axis=0), keys, 1, 1)
    step = 16

    def softmax(index, carry):
        at = pl.multiple_of(index * step, step)
        bias = bias_ref[pl.ds(pl.multiple_of(lax.rem(at, rows), step), step), :]
        scores = scores_ref[pl.ds(at, step), :] * (1.0 / math.sqrt(HD)) + bias
        exponent = jnp.exp(scores - jnp.max(scores, axis=1, keepdims=True))
        total = jnp.sum(exponent, axis=1, keepdims=True)
        probs_ref[pl.ds(at, step), :] = (exponent / total).astype(BF)
        return carry

    lax.fori_loop(0, heads * rows // step, softmax, 0, unroll=4)
    attended = dot(probs_ref[...], values, 1, 0).astype(BF)
    for head in range(heads):
        out_ref[:, head * HD : (head + 1) * HD] = attended[head * rows : (head + 1) * rows]


def attend(projected, prompt, piece, plan, events):
    rows = projected.shape[0] // 2
    cols = QH // 2 * HD
    pieces, _, prompt_dev, width = prompt.shape
    seen = PROMPT + piece.shape[1] - prompt_dev
    shape = jax.ShapeDtypeStruct((2 * rows, cols), BF)
    block = pl.BlockSpec((rows, cols), lambda b: (b, 0))
    table = pl.BlockSpec((rows, HD), lambda b: (0, 0))
    heads = cols // HD
    return pl.pallas_call(
        attend_kernel,
        grid=(2,),
        in_specs=[
            block,
            pl.BlockSpec((pieces, 1, prompt_dev, width), lambda b: (0, b, 0, 0)),
            pl.BlockSpec((1,) + piece.shape[1:], lambda b: (b, 0, 0)),
            pl.BlockSpec((rows, seen), lambda b: (0, 0)),
            table,
            table,
        ]
        + [pl.BlockSpec(memory_space=pl.ANY)] * len(events),
        out_specs=[block, block],
        out_shape=[shape, shape],
        scratch_shapes=[
            pltpu.VMEM((seen, width), BF),
            pltpu.VMEM((heads * rows, seen), F32),
            pltpu.VMEM((heads * rows, seen), BF),
        ],
        compiler_params=kernel_params(1),
        name="attend",
    )(projected, prompt, piece, plan["bias"], *plan["rope"], *events)


def attend_back_kernel(query_ref, grad_ref, prompt_ref, piece_ref, bias_ref, cos_ref, sin_ref, *refs):
    out_ref, prompt_out, piece_out, rows_ref, scores_ref, slopes_ref, probs_ref, dscores_ref = refs[-8:]
    rows, cols = query_ref.shape
    heads = cols // HD
    prompt_dev = prompt_ref.shape[2]
    pieces = prompt_ref.shape[0]
    scale = 1.0 / math.sqrt(HD)
    rows_ref[:PROMPT] = prompt_ref[...].reshape(PROMPT, 2 * HD)
    rows_ref[PROMPT:] = piece_ref[0, prompt_dev:]
    keys, values = rows_ref[:, :HD], rows_ref[:, HD:]
    split = [(head * HD, (head + 1) * HD) for head in range(heads)]
    queries = jnp.concatenate([query_ref[:, a:b] for a, b in split], axis=0)
    grads = jnp.concatenate([grad_ref[:, a:b] for a, b in split], axis=0)
    scores_ref[...] = dot(queries, keys, 1, 1)
    slopes_ref[...] = dot(grads, values, 1, 1)
    step = 16

    def softmax(index, carry):
        at = pl.multiple_of(index * step, step)
        bias = bias_ref[pl.ds(pl.multiple_of(lax.rem(at, rows), step), step), :]
        scores = scores_ref[pl.ds(at, step), :] * scale + bias
        exponent = jnp.exp(scores - jnp.max(scores, axis=1, keepdims=True))
        probs = exponent / jnp.sum(exponent, axis=1, keepdims=True)
        slopes = slopes_ref[pl.ds(at, step), :]
        delta = jnp.sum(probs * slopes, axis=1, keepdims=True)
        probs_ref[pl.ds(at, step), :] = probs.astype(BF)
        dscores_ref[pl.ds(at, step), :] = (probs * (slopes - delta)).astype(BF)
        return carry

    lax.fori_loop(0, heads * rows // step, softmax, 0, unroll=4)
    dscores = dscores_ref[...]
    grad_query = dot(dscores, keys, 1, 0) * scale
    cosine, sine = cos_ref[...], sin_ref[...]
    for head, (a, b) in enumerate(split):
        part = grad_query[head * rows : (head + 1) * rows]
        out_ref[:, a:b] = (part * cosine - pltpu.roll(part, HD // 2, 1) * sine).astype(BF)
    grad_keys = dot(dscores, queries, 0, 0) * scale
    grad_values = dot(probs_ref[...], grads, 0, 0)
    prompt_out[:, 0, :, :HD] = grad_keys[:PROMPT].reshape(pieces, prompt_dev, HD)
    prompt_out[:, 0, :, HD:] = grad_values[:PROMPT].reshape(pieces, prompt_dev, HD)
    piece_out[0, :, :HD] = grad_keys[PROMPT:]
    piece_out[0, :, HD:] = grad_values[PROMPT:]


def attend_back(queries, grad_attended, prompt, piece, plan, events):
    rows, cols = queries.shape[0] // 2, queries.shape[1]
    pieces, _, prompt_dev, width = prompt.shape
    own = piece.shape[1] - prompt_dev
    seen = PROMPT + own
    block = pl.BlockSpec((rows, cols), lambda b: (b, 0))
    table = pl.BlockSpec((rows, HD), lambda b: (0, 0))
    prompt_block = pl.BlockSpec((pieces, 1, prompt_dev, width), lambda b: (0, b, 0, 0))
    heads = cols // HD
    return pl.pallas_call(
        attend_back_kernel,
        grid=(2,),
        in_specs=[
            block,
            block,
            prompt_block,
            pl.BlockSpec((1,) + piece.shape[1:], lambda b: (b, 0, 0)),
            pl.BlockSpec((rows, seen), lambda b: (0, 0)),
            table,
            table,
        ]
        + [pl.BlockSpec(memory_space=pl.ANY)] * len(events),
        out_specs=[block, prompt_block, pl.BlockSpec((1, own, width), lambda b: (b, 0, 0))],
        out_shape=[
            jax.ShapeDtypeStruct(queries.shape, BF),
            jax.ShapeDtypeStruct(prompt.shape, F32),
            jax.ShapeDtypeStruct((2, own, width), F32),
        ],
        scratch_shapes=[
            pltpu.VMEM((seen, width), BF),
            pltpu.VMEM((heads * rows, seen), F32),
            pltpu.VMEM((heads * rows, seen), F32),
            pltpu.VMEM((heads * rows, seen), BF),
            pltpu.VMEM((heads * rows, seen), BF),
        ],
        compiler_params=kernel_params(1),
        name="attend_back",
    )(queries, grad_attended, prompt, piece, plan["bias"], *plan["rope"], *events)


def attention_forward(stream, weights, plan, events, fetch):
    rows = stream.shape[0]
    normed = norm_rows(stream, weights["gains"][0]).astype(BF)
    normed = to_staged(with_other(normed))
    projected = dot(normed, weights["qkv"], 1, 0)
    query_cols = QH // 2 * HD
    keys = rotate(projected[:, query_cols : query_cols + HD], plan["rope_both"], 1.0)
    values = projected[:, query_cols + HD : query_cols + 2 * HD]
    packed = jnp.concatenate([keys, values], axis=1).astype(BF).reshape(2, rows, 2 * HD)
    prompt, piece = key_value_gather(packed, plan["prompt_dev"])
    o_full = fetch(normed, piece, prompt)
    attended, queries = attend(projected, prompt, piece, plan, events)
    branch = from_staged(dot(attended, o_full, 1, 1))
    middle = stream + sum_with_other(branch)
    return middle, (normed, queries, prompt, piece, attended, o_full)


def attention_backward(grad_middle, stream, kept, weights, plan, events):
    normed, queries, prompt, piece, attended, o_full = kept
    rows = stream.shape[0]
    grad_branch = to_staged(with_other(grad_middle.astype(BF)))
    grad_attended = dot(grad_branch, o_full, 1, 0).astype(BF)
    grad_query, grad_prompt, grad_piece = attend_back(
        queries, grad_attended, prompt, piece, plan, events
    )
    grad_prompt = staged_reduce(grad_prompt)
    grad_square = jnp.concatenate(
        [dot(normed, grad_query, 0, 0), dot(grad_branch, attended, 0, 0)], axis=1
    ).astype(BF)
    grad_square = staged_panels(tie(grad_square, grad_prompt))
    grads = lanes_reduce(lanes_parts(jnp.concatenate([grad_prompt, grad_piece], axis=1), rows))
    grads = grads.reshape(2 * rows, 2 * HD)
    grad_keys = rotate(grads[:, :HD], plan["rope_both"], -1.0)
    grad_kv = jnp.concatenate([grad_keys, grads[:, HD:]], axis=1).astype(BF)
    grad_projected = jnp.concatenate([grad_query, grad_kv], axis=1)
    used = grad_projected.shape[1]
    grad_normed = dot(grad_projected, weights["qkv"][:, :used], 1, 1)
    grad_normed = sum_with_other(from_staged(grad_normed))
    grad_kv_weight = dot(normed, grad_kv, 0, 0)
    _, pull = jax.vjp(norm_rows, stream, weights["gains"][0])
    grad_stream, grad_gain = pull(grad_normed)
    return grad_stream + grad_middle, grad_square, grad_kv_weight, grad_gain


def route_masks(route_ids, experts, capacity):
    ids = jnp.arange(experts, dtype=jnp.int32)
    chosen = jnp.sum((route_ids[:, :, None] == ids[None, None, :]).astype(F32), axis=1)
    rows = route_ids.shape[0]
    ordinal = jnp.arange(rows, dtype=jnp.int32)
    before = (ordinal[:, None] > ordinal[None, :]).astype(BF)
    slots = dot(before, chosen.astype(BF), 1, 0)
    kept = jnp.where(slots < capacity, chosen, 0.0)
    return chosen.astype(BF), kept.astype(BF)


def gate_values(logits, chosen):
    masked = jnp.where(chosen > 0, logits, NEGATIVE)
    exponent = jnp.exp(masked - jnp.max(masked, axis=-1, keepdims=True))
    return exponent / jnp.sum(exponent, axis=-1, keepdims=True)


def gate_column(block_ref, width, expert):
    columns = block_ref[:, width:].astype(F32)
    hit = lax.broadcasted_iota(jnp.int32, columns.shape, 1) == expert
    return jnp.sum(jnp.where(hit, columns, 0.0), axis=1, keepdims=True)


def load_experts(weights_ref, held_ref, sems):
    lanes, _, three, units, _ = weights_ref.shape
    expert = pl.program_id(0)
    copies = [
        [
            pltpu.make_async_copy(
                weights_ref.at[lane, expert, index],
                held_ref.at[index, pl.ds(lane * units, units)],
                sems.at[index * lanes + lane],
            )
            for lane in range(lanes)
        ]
        for index in range(three)
    ]
    for group in copies:
        for copy in group:
            copy.start()

    def wait(index):
        for copy in copies[index]:
            copy.wait()

    return wait


def experts_kernel(expert_ref, block_ref, weights_ref, out_ref, held_ref, total_ref, sems):
    wait = load_experts(weights_ref, held_ref, sems)
    width = out_ref.shape[1]
    step = pl.program_id(0)
    scale = gate_column(block_ref, width, expert_ref[step])
    block = block_ref[:, :width]
    wait(0)
    gate = dot(block, held_ref[0], 1, 1)
    wait(1)
    up = dot(block, held_ref[1], 1, 1)
    weighted = (gelu_parts(gate)[0] * up * scale).astype(BF)
    wait(2)
    term = dot(weighted, held_ref[2], 1, 0)
    if total_ref is None:
        out_ref[...] = term.astype(out_ref.dtype)
    else:

        @pl.when(step == 0)
        def _():
            total_ref[...] = jnp.zeros_like(total_ref)

        total_ref[...] += term

        @pl.when(step == pl.num_programs(0) - 1)
        def _():
            out_ref[...] = total_ref[...].astype(out_ref.dtype)


def experts_scratch(weights, rows, columns):
    lanes, count, three, units, width = weights.shape
    return [
        pltpu.VMEM((three, lanes * units, width), BF),
        pltpu.VMEM((rows, columns), F32) if count > 1 else None,
        pltpu.SemaphoreType.DMA((three * lanes,)),
    ]


def experts_call(kernel, weights, rows, columns, **kwargs):
    scratch = experts_scratch(weights, rows, columns)
    if scratch[1] is None:
        inner = kernel

        def kernel(*refs):
            inner(*refs[:-1], None, refs[-1])

        scratch = [scratch[0], scratch[2]]
    return pl.pallas_call(
        kernel,
        grid=(weights.shape[1],),
        scratch_shapes=scratch,
        compiler_params=kernel_params(1),
        **kwargs,
    )


def experts_forward(block, weights, plan, dtype):
    rows = block.shape[0]
    width = weights.shape[-1]
    return experts_call(
        experts_kernel,
        weights,
        rows,
        width,
        in_specs=[
            pl.BlockSpec(memory_space=pltpu.SMEM),
            pl.BlockSpec((rows, width + 128), lambda e: (0, 0)),
            pl.BlockSpec(memory_space=pl.ANY),
        ],
        out_specs=pl.BlockSpec((rows, width), lambda e: (0, 0)),
        out_shape=jax.ShapeDtypeStruct((rows, width), dtype),
        name="experts",
    )(plan["experts"], block, weights)


def experts_back_kernel(expert_ref, block_ref, grad_ref, weights_ref, *refs):
    out_ref, gate_ref, up_ref, weighted_ref, *forward_ref = refs[:-3]
    held_ref, total_ref, sems = refs[-3:]
    wait = load_experts(weights_ref, held_ref, sems)
    width = grad_ref.shape[1]
    step = pl.program_id(0)
    expert = expert_ref[step]
    scale = gate_column(block_ref, width, expert)
    block = block_ref[:, :width]
    wait(0)
    gate = dot(block, held_ref[0], 1, 1)
    wait(1)
    up = dot(block, held_ref[1], 1, 1)
    wait(2)
    grad_raw = dot(grad_ref[...], held_ref[2], 1, 1)
    bent, slope = gelu_parts(gate)
    active = bent * up
    row_sum = jnp.sum(grad_raw * active, axis=1, keepdims=True)
    grad_active = grad_raw * scale
    grad_gate = (grad_active * up * slope).astype(BF)
    grad_up = (grad_active * bent).astype(BF)
    gate_ref[0] = grad_gate
    up_ref[0] = grad_up
    weighted = (active * scale).astype(BF)
    weighted_ref[0] = weighted
    if forward_ref:
        forward_ref[0][0] = dot(weighted, held_ref[2], 1, 0).astype(forward_ref[0].dtype)
    term = dot(grad_gate, held_ref[0], 1, 0) + dot(grad_up, held_ref[1], 1, 0)
    hit = lax.broadcasted_iota(jnp.int32, (block.shape[0], 128), 1) == expert
    gates = jnp.where(hit, row_sum, 0.0)
    if total_ref is None:
        out_ref[:, :width] = term.astype(out_ref.dtype)
        out_ref[:, width:] = gates.astype(out_ref.dtype)
    else:

        @pl.when(step == 0)
        def _():
            total_ref[...] = jnp.zeros_like(total_ref)

        total_ref[:, :width] += term
        total_ref[:, width:] += gates

        @pl.when(step == pl.num_programs(0) - 1)
        def _():
            out_ref[...] = total_ref[...].astype(out_ref.dtype)


def experts_back(block, grad, weights, plan, dtype, forward):
    rows = block.shape[0]
    lanes, count, _, units, width = weights.shape
    hidden = jax.ShapeDtypeStruct((count, rows, lanes * units), BF)
    hidden_spec = pl.BlockSpec((1, rows, lanes * units), lambda e: (e, 0, 0))
    row_spec = pl.BlockSpec((rows, width + 128), lambda e: (0, 0))
    out_specs = [row_spec] + [hidden_spec] * 3
    out_shape = [jax.ShapeDtypeStruct((rows, width + 128), dtype)] + [hidden] * 3
    if forward:
        out_specs.append(pl.BlockSpec((1, rows, width), lambda e: (e, 0, 0)))
        out_shape.append(jax.ShapeDtypeStruct((count, rows, width), dtype))
    return experts_call(
        experts_back_kernel,
        weights,
        rows,
        width + 128,
        in_specs=[
            pl.BlockSpec(memory_space=pltpu.SMEM),
            row_spec,
            pl.BlockSpec((rows, width), lambda e: (0, 0)),
            pl.BlockSpec(memory_space=pl.ANY),
        ],
        out_specs=out_specs,
        out_shape=out_shape,
        name="experts_back",
    )(plan["experts"], block, grad, weights)


def experts_weights_kernel(*refs):
    out_ref = refs[-1]
    sides = [refs[:5], refs[5:10]]
    lanes, _, _, units, width = out_ref.shape
    for index in range(3):

        @pl.when(pl.program_id(1) == index)
        def _(index=index):
            total = None
            for block_ref, grad_ref, *hidden_refs in sides:
                right = grad_ref[...] if index == 2 else block_ref[:, :width]
                term = dot(hidden_refs[index][0], right, 0, 0)
                total = term if total is None else total + term
            total = total.astype(BF)
            for lane in range(lanes):
                out_ref[lane, 0, 0] = total[lane * units : (lane + 1) * units]


def experts_weights(sides, weights, events):
    lanes, count, three, units, width = weights.shape
    rows = sides[0][0].shape[0]
    specs = [
        pl.BlockSpec((rows, width + 128), lambda e, j: (0, 0)),
        pl.BlockSpec((rows, width), lambda e, j: (0, 0)),
    ] + [pl.BlockSpec((1, rows, lanes * units), lambda e, j: (e, 0, 0))] * 3
    return pl.pallas_call(
        experts_weights_kernel,
        grid=(count, three),
        in_specs=specs + specs + [pl.BlockSpec(memory_space=pl.ANY)] * len(events),
        out_specs=pl.BlockSpec((lanes, 1, 1, units, width), lambda e, j: (0, e, j, 0, 0)),
        out_shape=jax.ShapeDtypeStruct(weights.shape, BF),
        compiler_params=kernel_params(2),
        name="experts_weights",
    )(*sides[0], *sides[1], *events)


def layer_backward(grad_out, grad_blocks, kept, weights, plan, events, forward):
    stream, attention_kept, middle, moe_in, blocks, chosen, within = kept
    other, *other_kept = experts_back(
        blocks[1], grad_blocks[1], weights["experts"], plan, BF, forward
    )
    mine, *mine_kept = experts_back(
        blocks[0], grad_blocks[0], weights["experts"], plan, F32, forward
    )
    terms = (mine_kept.pop(), other_kept.pop()) if forward else None
    grad_moe = rows_reduce(mine, other, stream.shape[0])
    expert_grads = experts_weights(
        ((blocks[0], grad_blocks[0], *mine_kept), (blocks[1], grad_blocks[1], *other_kept)),
        weights["experts"],
        events,
    )
    grad_moe = tie(grad_moe, expert_grads)
    event = grad_moe
    width = middle.shape[1]
    grad_gate = grad_moe[:, width : width + within.shape[1]] * within
    grad_moe = grad_moe[:, :width]
    gates = gate_values(dot(moe_in, weights["router"], 1, 0), chosen)
    grad_logits = gates * (grad_gate - jnp.sum(gates * grad_gate, axis=-1, keepdims=True))
    grad_logits = grad_logits.astype(BF)
    grad_moe = grad_moe + dot(grad_logits, weights["router"], 1, 1)
    grad_router = dot(moe_in, grad_logits, 0, 0)
    _, pull = jax.vjp(norm_rows, middle, weights["gains"][1])
    grad_middle, grad_gain_moe = pull(grad_moe)
    grad_middle = grad_middle + grad_out
    grad_stream, grad_square, grad_kv, grad_gain = attention_backward(
        grad_middle, stream, attention_kept, weights, plan, ()
    )
    extras = jnp.concatenate([grad_router, grad_gain[:, None], grad_gain_moe[:, None]], axis=1)
    grad_small = jnp.concatenate([grad_kv, from_dp(pad_columns(extras))], axis=1)
    return grad_stream, (grad_square, grad_small, expert_grads), (event, terms)


def pad_columns(values, columns=128):
    return jnp.pad(values, ((0, 0), (0, columns - values.shape[1])))


def from_dp(values):
    return to_staged(values.T).T


def holder():
    return (lax.axis_index("tensor") // 2) == lax.axis_index("section")


def head_columns(kv_weight, head):
    half = kv_weight.shape[1] // 2
    return jnp.concatenate(
        [kv_weight[:, head * HD : (head + 1) * HD], kv_weight[:, half + head * HD : half + (head + 1) * HD]],
        axis=1,
    )


def to_holders(own):
    lanes = lax.axis_size("tensor")
    pairs = [(t, lanes + t) for t in range(lanes // 2, lanes)]
    pairs += [(lanes + t, t) for t in range(lanes // 2)]
    moved = lax.ppermute(own, ("section", "tensor"), pairs)
    leading = lax.axis_index("section") == 0
    return jnp.where(leading, own, moved), jnp.where(leading, moved, own)


def from_holders(first, second):
    lanes = lax.axis_size("tensor")
    pairs = [(lanes + t, t) for t in range(lanes // 2, lanes)]
    pairs += [(t, lanes + t) for t in range(lanes // 2)]
    leading = lax.axis_index("section") == 0
    moved = lax.ppermute(jnp.where(leading, second, first), ("section", "tensor"), pairs)
    return jnp.where(holder(), jnp.where(leading, first, second), moved)


def reduce_small(parts):
    lanes = lax.axis_size("tensor")
    return lanes_reduce(parts.reshape(lanes, -1, parts.shape[1]))


def staged_panels(grads):
    pieces = lax.axis_size("dp")
    return staged_reduce(grads.reshape(pieces, -1, grads.shape[1]))


def per_device(edge_in, routes, q_weight, o_weight, kv_weight, router, gains, w_in, w_out):
    section = lax.axis_index("section")
    leading = section == 0
    lanes = lax.axis_size("tensor")
    pieces = lax.axis_size("dp")
    rows = edge_in.shape[2]
    piece_rows = rows * lanes
    prompt_dev = PROMPT // pieces
    local, units, width = w_out.shape[1:]
    experts = local * pieces
    top = routes.shape[3]
    capacity = lanes * (
        (9 * piece_rows * top + 8 * experts * lanes - 1) // (8 * experts * lanes)
    )

    edge_kept = lax.dynamic_index_in_dim(edge_in[0], section, 0, keepdims=False)
    edge_got = section_swap(lax.dynamic_index_in_dim(edge_in[0], 1 - section, 0, keepdims=False))
    stream = jnp.where(leading, edge_kept, edge_got).astype(F32)
    cotangent = jnp.where(leading, edge_got, edge_kept)
    route_kept = lax.dynamic_index_in_dim(routes[0], section, 0, keepdims=False)
    route_got = section_swap(lax.dynamic_index_in_dim(routes[0], 1 - section, 0, keepdims=False))
    route_first = jnp.where(leading, route_kept, route_got)
    route_second = jnp.where(leading, route_got, route_kept)

    share = local // 2
    pack = jnp.stack([w_in[0, :, 0], w_in[0, :, 1], w_out[0]], axis=1)
    pack_kept = lax.dynamic_slice_in_dim(pack, section * share, share, 0)
    pack_got = section_swap(lax.dynamic_slice_in_dim(pack, (1 - section) * share, share, 0))
    pack_first = jnp.where(leading, pack_kept, pack_got)
    pack_second = jnp.where(leading, pack_got, pack_kept)
    experts_first = lax.all_gather(pack_first, "tensor", axis=0, tiled=False)

    masks = [route_masks(ids, experts, capacity) for ids in (route_first, route_second)]
    masks = [
        [
            lax.dynamic_slice_in_dim(member, lax.axis_index("tensor") * rows, rows, 0).astype(F32)
            for member in pair
        ]
        for pair in masks
    ]
    squares = to_holders(jnp.stack([q_weight[0], o_weight[0]]))
    extras = pad_columns(jnp.concatenate([router[0], gains[0].T], axis=1))
    heads = [jnp.concatenate([head_columns(kv_weight[0], h), extras], axis=1) for h in range(2)]
    small_kept = jnp.where(leading, heads[0], heads[1])
    small_got = section_swap(jnp.where(leading, heads[1], heads[0]))
    smalls = lanes_gather(
        jnp.concatenate(
            [jnp.where(leading, small_kept, small_got), jnp.where(leading, small_got, small_kept)],
            axis=1,
        ),
        0,
    )
    small_cols = small_kept.shape[1]
    query_cols = QH // 2 * HD
    half = q_weight.shape[1]
    panel = jnp.concatenate([holders_gather(squares[0][0]), smalls[:, :small_cols]], axis=1)
    qkv_first = staged_gather(tie(panel, pack_first)).reshape(width, -1)

    def layer_weights(layer, qkv):
        extras = from_staged(qkv[:, query_cols + 2 * HD :], 0)
        return {
            "qkv": qkv,
            "router": extras[:, :experts],
            "gains": extras[:, experts : experts + 2].T.astype(F32),
        }

    piece_index = lax.axis_index("dp")
    tables = rope_tables(own_places(rows, prompt_dev))
    plan = {
        "prompt_dev": prompt_dev,
        "rope": tables,
        "rope_both": [jnp.concatenate([table, table], axis=0) for table in tables],
        "bias": jnp.where(allowed_pairs(rows, piece_rows, prompt_dev), 0.0, NEGATIVE),
        "experts": piece_index * local + section * share + jnp.arange(share, dtype=jnp.int32),
    }
    def experts_rows(layer, middle):
        moe_in = norm_rows(middle, weights[layer]["gains"][1]).astype(BF)
        chosen, within = masks[layer]
        gates = gate_values(dot(moe_in, weights[layer]["router"], 1, 0), chosen) * within
        moe_rows = jnp.concatenate([moe_in, pad_columns(gates.astype(BF))], axis=1)
        return moe_in, rows_gather(moe_rows)

    weights = [layer_weights(0, qkv_first), None]
    weights[0]["experts"] = experts_first

    def fetch_first(normed, piece, prompt):
        o_first = holders_gather(tie(squares[0][1], panel), normed)
        return staged_gather(o_first, (piece, prompt)).reshape(width, -1)

    middle_first, attention_first = attention_forward(
        stream, weights[0], plan, (), fetch_first
    )
    attended = attention_first[4]
    moe_first, blocks_first = experts_rows(0, middle_first)
    q_second = holders_gather(tie(squares[1][0], attended), blocks_first[0])
    mine = experts_forward(blocks_first[0], experts_first, plan, F32)
    other = experts_forward(blocks_first[1], experts_first, plan, BF)
    result = middle_first + rows_reduce(mine, other, rows)
    hidden = result.astype(BF).astype(F32)
    panel = jnp.concatenate([q_second, smalls[:, small_cols:]], axis=1)
    qkv_second = staged_gather(panel, (other, result)).reshape(width, -1)
    o_second = holders_gather(tie(squares[1][1], blocks_first[0]), result)

    weights[1] = layer_weights(1, qkv_second)
    weights[1]["experts"] = lax.all_gather(
        tie(pack_second, blocks_first[0]), "tensor", axis=0, tiled=False
    )
    grad_blocks = []

    def fetch_second(normed, piece, prompt):
        grad_blocks.extend(rows_gather(tie(cotangent, prompt)))
        return staged_gather(tie(o_second, normed), (piece, prompt)).reshape(width, -1)

    middle_second, attention_second = attention_forward(
        hidden, weights[1], plan, (), fetch_second
    )
    moe_second, blocks_second = experts_rows(1, middle_second)

    grads = [None, None]
    kept = (stream, attention_first, middle_first, moe_first, blocks_first, *masks[0])
    kept_second = (hidden, attention_second, middle_second, moe_second, blocks_second, *masks[1])
    grad_stream, grads[1], (event, terms) = layer_backward(
        cotangent.astype(F32), grad_blocks, kept_second, weights[1], plan, (), True
    )
    grad_out = grad_stream.astype(BF)
    grad_blocks = rows_gather(grad_out)
    square = tie(grads[1][0], grad_blocks[0])
    square_second = holders_reduce(
        jnp.concatenate([square[:, :query_cols], square[:, query_cols:]], axis=0)
    )
    small_second = reduce_small(staged_panels(tie(grads[1][1], grad_blocks[0])))
    terms = [jnp.sum(term, axis=0) for term in terms]
    result = middle_second + rows_reduce(*tie(tuple(terms), grad_blocks[1]), rows)
    grad_stream, grads[0], _ = layer_backward(
        grad_out.astype(F32),
        grad_blocks,
        kept,
        weights[0],
        plan,
        (square_second, small_second),
        False,
    )

    edge_kept = jnp.where(leading, grad_stream, result)
    edge_got = section_swap(jnp.where(leading, result, grad_stream))
    edge_out = jnp.where(
        leading, jnp.stack([edge_kept, edge_got]), jnp.stack([edge_got, edge_kept])
    )

    grad_square, grad_small, _ = grads[0]
    half = grad_square.shape[0]
    square_first = holders_reduce(
        jnp.concatenate([grad_square[:, :query_cols], grad_square[:, query_cols:]], axis=0)
    )
    small_first = reduce_small(staged_panels(grad_small))
    both = from_holders(square_first, square_second)
    grad_q, grad_o = both[:half], both[half:]
    small_kept = jnp.where(leading, small_first, small_second)
    small_got = section_swap(jnp.where(leading, small_second, small_first))
    key_values = jnp.where(
        leading,
        jnp.stack([small_kept[:, : 2 * HD], small_got[:, : 2 * HD]]),
        jnp.stack([small_got[:, : 2 * HD], small_kept[:, : 2 * HD]]),
    )
    grad_kv = jnp.concatenate(
        [key_values[0, :, :HD], key_values[1, :, :HD], key_values[0, :, HD:], key_values[1, :, HD:]],
        axis=1,
    )
    extras = small_kept[:, 2 * HD :] + small_got[:, 2 * HD :]

    summed = [
        lax.psum_scatter(grads[layer][2], "tensor", scatter_dimension=0, tiled=False)
        for layer in range(2)
    ]
    second_got = section_send(summed[1], 0)
    first_got = section_send(summed[0], 1)
    grad_experts = jnp.concatenate(
        [jnp.where(leading, summed[0], second_got), jnp.where(leading, first_got, summed[1])],
        axis=0,
    ).astype(F32)
    return (
        edge_out[None],
        grad_q[None],
        grad_o[None],
        grad_kv[None],
        extras[None, :, :experts],
        extras[:, experts : experts + 2].T[None],
        grad_experts[None, :, :2],
        grad_experts[None, :, 2],
    )


def solution(mesh):
    placed = (
        P("section", None, ("dp", "tensor"), None),
        P("section", None, "dp", None),
        P("section", "dp", "tensor"),
        P("section", "dp", "tensor"),
        P("section", ("dp", "tensor"), None),
        P("section", ("dp", "tensor"), None),
        P("section", None, ("dp", "tensor")),
        P("section", "dp", None, "tensor", None),
        P("section", "dp", "tensor", None),
    )
    return jax.shard_map(
        per_device,
        mesh=mesh,
        in_specs=placed,
        out_specs=(placed[0],) + placed[2:],
        check_vma=False,
    )
```

```python
import functools
import math

import jax
import jax.numpy as jnp
from jax import lax
from jax.experimental import pallas as pl
from jax.experimental.pallas import tpu as pltpu
from jax.sharding import PartitionSpec as P

QH = 12
KVH = 2
HD = 128
PROMPT = 1024
CONT = 256

EPSILON = 1e-06
NEGATIVE = -1e30
ROPE_BASE = 10000.0
BF = jnp.bfloat16
F32 = jnp.float32
VMEM_BYTES = 56 * 1024 * 1024
ROWS_HELD = 512
GELU_SCALE = math.sqrt(2.0 / math.pi)
GELU_CUBE = 0.044715


def dot(left, right, left_axis, right_axis):
    return lax.dot_general(
        left, right, (((left_axis,), (right_axis,)), ((), ())), preferred_element_type=F32
    )


def norm_rows(values, gain):
    return values * lax.rsqrt(jnp.mean(values * values, axis=-1, keepdims=True) + EPSILON) * gain


def gelu_parts(values):
    square = values * values
    bent = jnp.tanh(GELU_SCALE * values * (1.0 + GELU_CUBE * square))
    half = 0.5 * (1.0 + bent)
    slope = half + 0.5 * values * (1.0 - bent * bent) * (
        GELU_SCALE * (1.0 + 3.0 * GELU_CUBE * square)
    )
    return values * half, slope


def kernel_params(axes):
    return pltpu.CompilerParams(
        vmem_limit_bytes=VMEM_BYTES,
        dimension_semantics=("arbitrary",) * axes if axes else None,
    )


def tree_swap(values, axis, pairs):
    return jax.tree.map(lambda v: lax.ppermute(v, axis, pairs), values)


def section_swap(values):
    return tree_swap(values, "section", [(0, 1), (1, 0)])


def section_send(values, source):
    return tree_swap(values, "section", [(source, 1 - source)])


def dp_bits():
    return lax.axis_size("dp").bit_length() - 1


def stage_bit(section, stage):
    return stage if section == 0 else dp_bits() - 1 - stage


def stage_swap(values, stage):
    count = lax.axis_size("dp")
    pairs = [
        (s * count + d, s * count + (d ^ (1 << stage_bit(s, stage))))
        for s in range(2)
        for d in range(count)
    ]
    return lax.ppermute(values, ("section", "dp"), pairs)


def stage_origin(position):
    origins = []
    for section in range(2):
        moved = jnp.int32(0)
        for stage in range(dp_bits()):
            moved = moved | ((position >> stage) & 1) << stage_bit(section, stage)
        origins.append(moved)
    return lax.axis_index("dp") ^ jnp.where(lax.axis_index("section") == 0, *origins)


def stage_position(origin):
    moved = origin ^ lax.axis_index("dp")
    positions = []
    for section in range(2):
        position = jnp.int32(0)
        for stage in range(dp_bits()):
            position = position | ((moved >> stage_bit(section, stage)) & 1) << stage
        positions.append(position)
    return jnp.where(lax.axis_index("section") == 0, *positions)


def stage_join(block, stage, until):
    moved = stage_swap(block, stage)
    if until is not None:
        moved = tie(moved, until)
    return jnp.concatenate([block, moved], axis=0)


def staged_gather(block, until=()):
    block = block[None]
    for stage in range(dp_bits()):
        block = stage_join(block, stage, until[min(stage, len(until) - 1)] if until else None)
    return block


def staged_reduce(parts, since=(), until=()):
    for turn, stage in enumerate(reversed(range(dp_bits()))):
        half = parts.shape[0] // 2
        leaving = parts[half:].astype(BF)
        if since and since[min(turn, len(since) - 1)] is not None:
            leaving = tie(leaving, since[min(turn, len(since) - 1)])
        arrived = stage_swap(leaving, stage)
        if until and until[min(turn, len(until) - 1)] is not None:
            arrived = tie(arrived, until[min(turn, len(until) - 1)])
        parts = parts[:half].astype(F32) + arrived.astype(F32)
    return parts[0].astype(F32)


def reduce_stage(parts, stage, until):
    half = parts.shape[0] // 2
    arrived = tie(stage_swap(parts[half:].astype(BF), stage), until)
    return parts[:half].astype(F32) + arrived.astype(F32)


def reduce_rest(parts):
    for stage in reversed(range(dp_bits() - 1)):
        half = parts.shape[0] // 2
        arrived = stage_swap(parts[half:].astype(BF), stage)
        parts = parts[:half] + arrived.astype(F32)
    return parts[0]


def to_staged(blocks):
    return jnp.concatenate(
        [
            lax.dynamic_slice_in_dim(blocks, stage_origin(jnp.int32(p)), 1, 0)
            for p in range(blocks.shape[0])
        ],
        axis=0,
    )


def from_staged(blocks):
    blocks = jnp.concatenate(
        [
            lax.dynamic_slice_in_dim(blocks, stage_position(jnp.int32(d)), 1, 0)
            for d in range(blocks.shape[0])
        ],
        axis=0,
    )
    return blocks.reshape(-1, blocks.shape[-1])


def mirrored():
    here = lax.axis_index("tensor")
    return jnp.where(lax.axis_index("section") == 0, here, lax.axis_size("tensor") - 1 - here)


def mirrored_send(values, pairs):
    lanes = lax.axis_size("tensor")
    routes = [(a, b) for a, b in pairs]
    routes += [(2 * lanes - 1 - a, 2 * lanes - 1 - b) for a, b in pairs]
    return lax.ppermute(values, ("section", "tensor"), routes)


def holders_gather(block, until=None):
    place = mirrored()
    near = mirrored_send(block, [(0, 1), (1, 2)])
    far = mirrored_send(block, [(0, 2), (1, 3)])
    last = mirrored_send(block, [(0, 3), (1, 0)])
    if until is not None:
        near, far, last = tie((near, far, last), until)
    outer = jnp.where(
        place == 0, block, jnp.where(place == 1, near, jnp.where(place == 2, far, last))
    )
    inner = jnp.where(
        place == 0, last, jnp.where(place == 1, block, jnp.where(place == 2, near, far))
    )
    leading = lax.axis_index("section") == 0
    return jnp.concatenate(
        [jnp.where(leading, outer, inner), jnp.where(leading, inner, outer)], axis=1
    )


def holders_reduce(parts, until=None):
    place = mirrored()
    leading = lax.axis_index("section") == 0
    cols = parts.shape[1] // 2
    outer = jnp.where(leading, parts[:, :cols], parts[:, cols:])
    inner = jnp.where(leading, parts[:, cols:], parts[:, :cols])
    total = jnp.where(place == 0, outer, inner)
    outer, inner = outer.astype(BF), inner.astype(BF)
    near = mirrored_send(jnp.where(place == 1, outer, inner), [(1, 0), (2, 1)])
    far = mirrored_send(jnp.where(place == 2, outer, inner), [(2, 0), (3, 1)])
    last = mirrored_send(jnp.where(place == 3, outer, inner), [(3, 0), (0, 1)])
    if until is not None:
        near, far, last = tie((near, far, last), until)
    return total + near.astype(F32) + far.astype(F32) + last.astype(F32)


def lanes_gather(block, axis, until=None):
    lanes = lax.axis_size("tensor")
    here = lax.axis_index("tensor")
    blocks = [block]
    for apart in range(1, lanes):
        blocks.append(
            lax.ppermute(block, "tensor", [(i, (i - apart) % lanes) for i in range(lanes)])
        )
    if until is not None:
        blocks[1:] = tie(blocks[1:], until)
    size = block.shape[axis]
    return lax.dynamic_slice_in_dim(
        jnp.concatenate(blocks + blocks[: lanes - 1], axis=axis),
        jnp.where(here == 0, 0, lanes - here) * size,
        lanes * size,
        axis,
    )


def lanes_reduce(parts, until=None):
    lanes = lax.axis_size("tensor")
    here = lax.axis_index("tensor")
    total = lax.dynamic_index_in_dim(parts, here, 0, keepdims=False)
    for apart in range(1, lanes):
        term = lax.dynamic_index_in_dim(parts, (here + apart) % lanes, 0, keepdims=False)
        pairs = [(i, (i + apart) % lanes) for i in range(lanes)]
        arrived = lax.ppermute(term.astype(BF), "tensor", pairs)
        if until is not None:
            arrived = tie(arrived, until)
        total = total + arrived.astype(F32)
    return total


def tie(values, *events):
    probe = sum(event[(0,) * event.ndim].astype(F32) for event in events)
    return jax.tree.map(lambda v: jnp.where(probe != probe, jnp.zeros((), v.dtype), v), values)


def rows_gather(block):
    mine = staged_gather(block).reshape(-1, block.shape[1])
    return mine, section_swap(mine)


def rows_reduce(mine, other, rows, until=None):
    arrived = section_swap(other.astype(BF))
    if until is not None:
        arrived = tie(arrived, until[0])
    total = mine + arrived.astype(F32)
    return staged_reduce(
        total.reshape(-1, rows, total.shape[1]), until=until[1:] if until is not None else ()
    )


def rope_tables(places):
    half = HD // 2
    frequency = jnp.exp(jnp.arange(half, dtype=F32) * (-math.log(ROPE_BASE) / half))
    angles = places.astype(F32)[:, None] * frequency[None, :]
    cosine, sine = jnp.cos(angles), jnp.sin(angles)
    return (
        jnp.concatenate([cosine, cosine], axis=1),
        jnp.concatenate([-sine, sine], axis=1),
    )


def rotate(values, tables, sign):
    half = HD // 2
    turned = jnp.concatenate([values[:, half:], values[:, :half]], axis=1)
    return values * tables[0] + turned * (sign * tables[1])


def key_value_gather(key_value, prompt_dev):
    piece = lanes_gather(key_value, 1)
    return staged_gather(piece[:, :prompt_dev]), piece


def lanes_parts(piece, rows):
    batches, _, width = piece.shape
    return piece.reshape(batches, -1, rows, width).transpose(1, 0, 2, 3)


def allowed_pairs(rows, piece_rows, prompt_dev):
    piece_index = lax.axis_index("dp")
    ordinal = lax.axis_index("tensor") * rows + jnp.arange(rows, dtype=jnp.int32)
    columns = jnp.arange(PROMPT + piece_rows - prompt_dev, dtype=jnp.int32)
    key_place = stage_origin(columns // prompt_dev) * prompt_dev + columns % prompt_dev
    query_prompt = ordinal < prompt_dev
    query_place = piece_index * prompt_dev + ordinal
    query_cont = (ordinal - prompt_dev) // CONT
    query_step = (ordinal - prompt_dev) % CONT
    local_col = columns - PROMPT
    prompt_part = jnp.logical_or(
        jnp.logical_not(query_prompt)[:, None], key_place[None, :] <= query_place[:, None]
    )
    cont_part = jnp.logical_and(
        jnp.logical_not(query_prompt)[:, None],
        jnp.logical_and(
            local_col[None, :] // CONT == query_cont[:, None],
            local_col[None, :] % CONT <= query_step[:, None],
        ),
    )
    return jnp.where((columns < PROMPT)[None, :], prompt_part, cont_part)


def own_places(rows, prompt_dev):
    piece_index = lax.axis_index("dp")
    ordinal = lax.axis_index("tensor") * rows + jnp.arange(rows, dtype=jnp.int32)
    return jnp.where(
        ordinal < prompt_dev,
        piece_index * prompt_dev + ordinal,
        PROMPT + (ordinal - prompt_dev) % CONT,
    )


def with_other(values):
    return jnp.concatenate([values, section_swap(values)], axis=0)


def sum_with_other(values):
    rows = values.shape[0] // 2
    return values[:rows] + section_swap(values[rows:].astype(BF)).astype(F32)


def attend_kernel(query_ref, prompt_ref, piece_ref, bias_ref, cos_ref, sin_ref, *refs):
    out_ref, queries_ref, rows_ref, scores_ref, probs_ref = refs[-5:]
    rows, cols = query_ref.shape
    heads = cols // HD
    prompt_dev = prompt_ref.shape[2]
    seen = rows_ref.shape[0]
    rows_ref[:PROMPT] = prompt_ref[...].reshape(PROMPT, 2 * HD)
    rows_ref[PROMPT:] = piece_ref[0, prompt_dev:]
    cosine, sine = cos_ref[...], sin_ref[...]
    queries = []
    for head in range(heads):
        part = query_ref[:, head * HD : (head + 1) * HD]
        part = part * cosine + pltpu.roll(part, HD // 2, 1) * sine
        part = part.astype(BF)
        queries_ref[:, head * HD : (head + 1) * HD] = part
        queries.append(part)
    keys, values = rows_ref[:, :HD], rows_ref[:, HD:]
    scores_ref[...] = dot(jnp.concatenate(queries, axis=0), keys, 1, 1)
    step = rows

    def softmax(index, carry):
        at = pl.multiple_of(index * step, step)
        bias = bias_ref[...]
        scores = scores_ref[pl.ds(at, step), :] * (1.0 / math.sqrt(HD)) + bias
        exponent = jnp.exp(scores - jnp.max(scores, axis=1, keepdims=True))
        total = jnp.sum(exponent, axis=1, keepdims=True)
        probs_ref[pl.ds(at, step), :] = (exponent / total).astype(BF)
        return carry

    lax.fori_loop(0, heads, softmax, 0, unroll=2)
    attended = dot(probs_ref[...], values, 1, 0).astype(BF)
    for head in range(heads):
        out_ref[:, head * HD : (head + 1) * HD] = attended[head * rows : (head + 1) * rows]


def attend(projected, prompt, piece, plan, events):
    rows = projected.shape[0] // 2
    cols = QH // 2 * HD
    pieces, _, prompt_dev, width = prompt.shape
    seen = PROMPT + piece.shape[1] - prompt_dev
    shape = jax.ShapeDtypeStruct((2 * rows, cols), BF)
    block = pl.BlockSpec((rows, cols), lambda b: (b, 0))
    table = pl.BlockSpec((rows, HD), lambda b: (0, 0))
    heads = cols // HD
    return pl.pallas_call(
        attend_kernel,
        grid=(2,),
        in_specs=[
            block,
            pl.BlockSpec((pieces, 1, prompt_dev, width), lambda b: (0, b, 0, 0)),
            pl.BlockSpec((1,) + piece.shape[1:], lambda b: (b, 0, 0)),
            pl.BlockSpec((rows, seen), lambda b: (0, 0)),
            table,
            table,
        ]
        + [pl.BlockSpec(memory_space=pl.ANY)] * len(events),
        out_specs=[block, block],
        out_shape=[shape, shape],
        scratch_shapes=[
            pltpu.VMEM((seen, width), BF),
            pltpu.VMEM((heads * rows, seen), F32),
            pltpu.VMEM((heads * rows, seen), BF),
        ],
        compiler_params=kernel_params(1),
        name="attend",
    )(projected, prompt, piece, plan["bias"], *plan["rope"], *events)


def attend_back_kernel(query_ref, grad_ref, prompt_ref, piece_ref, bias_ref, cos_ref, sin_ref, *refs):
    out_ref, prompt_out, piece_out, rows_ref, scores_ref, slopes_ref, probs_ref, dscores_ref = refs[-8:]
    rows, cols = query_ref.shape
    heads = cols // HD
    prompt_dev = prompt_ref.shape[2]
    pieces = prompt_ref.shape[0]
    scale = 1.0 / math.sqrt(HD)
    rows_ref[:PROMPT] = prompt_ref[...].reshape(PROMPT, 2 * HD)
    rows_ref[PROMPT:] = piece_ref[0, prompt_dev:]
    keys, values = rows_ref[:, :HD], rows_ref[:, HD:]
    split = [(head * HD, (head + 1) * HD) for head in range(heads)]
    queries = jnp.concatenate([query_ref[:, a:b] for a, b in split], axis=0)
    grads = jnp.concatenate([grad_ref[:, a:b] for a, b in split], axis=0)
    scores_ref[...] = dot(queries, keys, 1, 1)
    slopes_ref[...] = dot(grads, values, 1, 1)
    step = rows

    def softmax(index, carry):
        at = pl.multiple_of(index * step, step)
        bias = bias_ref[...]
        scores = scores_ref[pl.ds(at, step), :] * scale + bias
        exponent = jnp.exp(scores - jnp.max(scores, axis=1, keepdims=True))
        probs = exponent / jnp.sum(exponent, axis=1, keepdims=True)
        slopes = slopes_ref[pl.ds(at, step), :]
        delta = jnp.sum(probs * slopes, axis=1, keepdims=True)
        probs_ref[pl.ds(at, step), :] = probs.astype(BF)
        dscores_ref[pl.ds(at, step), :] = (probs * (slopes - delta)).astype(BF)
        return carry

    lax.fori_loop(0, heads, softmax, 0, unroll=2)
    dscores = dscores_ref[...]
    grad_query = dot(dscores, keys, 1, 0) * scale
    cosine, sine = cos_ref[...], sin_ref[...]
    for head, (a, b) in enumerate(split):
        part = grad_query[head * rows : (head + 1) * rows]
        out_ref[:, a:b] = (part * cosine - pltpu.roll(part, HD // 2, 1) * sine).astype(BF)
    grad_keys = dot(dscores, queries, 0, 0) * scale
    grad_values = dot(probs_ref[...], grads, 0, 0)
    prompt_out[:, 0, :, :HD] = grad_keys[:PROMPT].reshape(pieces, prompt_dev, HD)
    prompt_out[:, 0, :, HD:] = grad_values[:PROMPT].reshape(pieces, prompt_dev, HD)
    piece_out[0, :, :HD] = grad_keys[PROMPT:]
    piece_out[0, :, HD:] = grad_values[PROMPT:]


def attend_back(queries, grad_attended, prompt, piece, plan, events):
    rows, cols = queries.shape[0] // 2, queries.shape[1]
    pieces, _, prompt_dev, width = prompt.shape
    own = piece.shape[1] - prompt_dev
    seen = PROMPT + own
    block = pl.BlockSpec((rows, cols), lambda b: (b, 0))
    table = pl.BlockSpec((rows, HD), lambda b: (0, 0))
    prompt_block = pl.BlockSpec((pieces, 1, prompt_dev, width), lambda b: (0, b, 0, 0))
    heads = cols // HD
    return pl.pallas_call(
        attend_back_kernel,
        grid=(2,),
        in_specs=[
            block,
            block,
            prompt_block,
            pl.BlockSpec((1,) + piece.shape[1:], lambda b: (b, 0, 0)),
            pl.BlockSpec((rows, seen), lambda b: (0, 0)),
            table,
            table,
        ]
        + [pl.BlockSpec(memory_space=pl.ANY)] * len(events),
        out_specs=[block, prompt_block, pl.BlockSpec((1, own, width), lambda b: (b, 0, 0))],
        out_shape=[
            jax.ShapeDtypeStruct(queries.shape, BF),
            jax.ShapeDtypeStruct(prompt.shape, F32),
            jax.ShapeDtypeStruct((2, own, width), F32),
        ],
        scratch_shapes=[
            pltpu.VMEM((seen, width), BF),
            pltpu.VMEM((heads * rows, seen), F32),
            pltpu.VMEM((heads * rows, seen), F32),
            pltpu.VMEM((heads * rows, seen), BF),
            pltpu.VMEM((heads * rows, seen), BF),
        ],
        compiler_params=kernel_params(1),
        name="attend_back",
    )(queries, grad_attended, prompt, piece, plan["bias"], *plan["rope"], *events)


def attention_forward(stream, weights, plan, events, fetch):
    rows = stream.shape[0]
    normed = norm_rows(stream, weights["gains"][0]).astype(BF)
    normed = with_other(normed)
    projected = dot(normed, weights["qkv"], 1, 0)
    query_cols = QH // 2 * HD
    keys = rotate(projected[:, query_cols : query_cols + HD], plan["rope_both"], 1.0)
    values = projected[:, query_cols + HD : query_cols + 2 * HD]
    packed = jnp.concatenate([keys, values], axis=1).astype(BF).reshape(2, rows, 2 * HD)
    prompt, piece = key_value_gather(packed, plan["prompt_dev"])
    o_full = fetch(normed, piece, prompt)
    attended, queries = attend(projected, prompt, piece, plan, events)
    middle = stream + sum_with_other(dot(attended, o_full, 1, 1))
    return middle, (normed, queries, prompt, piece, attended, o_full)


def attention_backward(grad_middle, stream, kept, weights, plan, events):
    normed, queries, prompt, piece, attended, o_full = kept
    rows = stream.shape[0]
    grad_branch = with_other(grad_middle.astype(BF))
    grad_attended = dot(grad_branch, o_full, 1, 0).astype(BF)
    grad_o = panels(dot(grad_branch, attended, 0, 0))
    grad_query, grad_prompt, grad_piece = attend_back(
        queries, grad_attended, prompt, piece, plan, events
    )
    grad_prompt = staged_reduce(grad_prompt)
    grad_q = panels(dot(normed, grad_query, 0, 0))
    grads = lanes_reduce(lanes_parts(jnp.concatenate([grad_prompt, grad_piece], axis=1), rows))
    grad_o = staged_reduce(grad_o, (None, grad_prompt), (grad_query, grads))
    grads = grads.reshape(2 * rows, 2 * HD)
    grad_keys = rotate(grads[:, :HD], plan["rope_both"], -1.0)
    grad_kv = jnp.concatenate([grad_keys, grads[:, HD:]], axis=1).astype(BF)
    grad_projected = jnp.concatenate([grad_query, grad_kv], axis=1)
    used = grad_projected.shape[1]
    grad_normed = dot(grad_projected, weights["qkv"][:, :used], 1, 1)
    grad_normed = sum_with_other(grad_normed)
    grad_q = staged_reduce(grad_q, (grad_prompt, None), (grads, grad_normed))
    grad_kv_weight = dot(normed, grad_kv, 0, 0)
    _, pull = jax.vjp(norm_rows, stream, weights["gains"][0])
    grad_stream, grad_gain = pull(grad_normed)
    return grad_stream + grad_middle, grad_q, grad_o, grad_kv_weight, grad_gain


def route_masks(route_ids, experts, capacity):
    ids = jnp.arange(experts, dtype=jnp.int32)
    chosen = jnp.sum((route_ids[:, :, None] == ids[None, None, :]).astype(F32), axis=1)
    rows = route_ids.shape[0]
    ordinal = jnp.arange(rows, dtype=jnp.int32)
    before = (ordinal[:, None] > ordinal[None, :]).astype(BF)
    slots = dot(before, chosen.astype(BF), 1, 0)
    kept = jnp.where(slots < capacity, chosen, 0.0)
    return chosen.astype(BF), kept.astype(BF)


def gate_values(logits, chosen):
    masked = jnp.where(chosen > 0, logits, NEGATIVE)
    exponent = jnp.exp(masked - jnp.max(masked, axis=-1, keepdims=True))
    return exponent / jnp.sum(exponent, axis=-1, keepdims=True)


def gate_column(block_ref, width, expert):
    columns = block_ref[:, width:].astype(F32)
    hit = lax.broadcasted_iota(jnp.int32, columns.shape, 1) == expert
    return jnp.sum(jnp.where(hit, columns, 0.0), axis=1, keepdims=True)


def experts_kernel(expert_ref, mine_ref, other_ref, weights_ref, mine_out, other_out, blocks_ref, held_ref, left_ref, right_ref, sems):
    lanes, count, three, units, _ = weights_ref.shape
    width = held_ref.shape[-1]
    used = iter(range(sems.shape[0]))

    def start(source, target):
        copy = pltpu.make_async_copy(source, target, sems.at[next(used)])
        copy.start()
        return copy

    rows = {}
    leaving = []
    for expert in range(count):
        arriving = []
        for index in range(three):
            arriving.append(
                [
                    start(
                        weights_ref.at[lane, expert, index],
                        held_ref.at[index, pl.ds(lane * units, units)],
                    )
                    for lane in range(lanes)
                ]
            )
            if expert == 0 and index < 2:
                rows[1 - index] = start((mine_ref, other_ref)[1 - index], blocks_ref.at[1 - index])
        for side, total_ref, out_ref in ((1, right_ref, other_out), (0, left_ref, mine_out)):
            block_ref = blocks_ref.at[side]
            if expert == 0:
                rows[side].wait()
            scale = gate_column(block_ref, width, expert_ref[expert])
            hidden = []
            for index in range(2):
                if side == 1:
                    for copy in arriving[index]:
                        copy.wait()
                hidden.append(dot(block_ref[:, :width], held_ref[index], 1, 1))
            weighted = (gelu_parts(hidden[0])[0] * hidden[1] * scale).astype(BF)
            if side == 1:
                for copy in arriving[2]:
                    copy.wait()
            term = dot(weighted, held_ref[2], 1, 0)
            if expert > 0:
                term = term + total_ref[...].astype(F32)
            total_ref[...] = term.astype(total_ref.dtype)
            if expert == count - 1:
                leaving.append(start(total_ref, out_ref))
    for copy in leaving:
        copy.wait()


def experts_forward(blocks, weights, plan):
    found = by_parts(lambda some: experts_forward_part(some, weights, plan), blocks)
    return [jnp.concatenate(members, axis=0) if len(members) > 1 else members[0] for members in zip(*found)]


def experts_forward_part(blocks, weights, plan):
    lanes, count, three, units, width = weights.shape
    rows = blocks[0].shape[0]
    anywhere = pl.BlockSpec(memory_space=pl.ANY)
    return pl.pallas_call(
        experts_kernel,
        in_specs=[pl.BlockSpec(memory_space=pltpu.SMEM)] + [anywhere] * 3,
        out_specs=[anywhere] * 2,
        out_shape=[
            jax.ShapeDtypeStruct((rows, width), F32),
            jax.ShapeDtypeStruct((rows, width), BF),
        ],
        scratch_shapes=[
            pltpu.VMEM((2, rows, width + 128), BF),
            pltpu.VMEM((three, lanes * units, width), BF),
            pltpu.VMEM((rows, width), F32),
            pltpu.VMEM((rows, width), BF),
            pltpu.SemaphoreType.DMA((4 + three * lanes * count,)),
        ],
        compiler_params=kernel_params(0),
        name="experts",
    )(plan["experts"], *blocks, weights)


def experts_back_kernel(forward, events, expert_ref, *refs):
    inputs, refs = refs[:5], refs[5 + events :]
    weights_ref = inputs[4]
    outs, refs = refs[: 5 if forward else 3], refs[5 if forward else 3 :]
    blocks_ref, grads_ref, held_ref, mine_ref, other_ref, hidden_ref, weight_ref = refs[:7]
    terms_refs, sems = refs[7:-1], refs[-1]
    lanes, count, _, units, _ = weights_ref.shape
    width = grads_ref.shape[-1]
    used = iter(range(sems.shape[0]))

    def start(source, target):
        copy = pltpu.make_async_copy(source, target, sems.at[next(used)])
        copy.start()
        return copy

    def load(expert, index):
        return [
            start(
                weights_ref.at[lane, expert, index],
                held_ref.at[index, pl.ds(lane * units, units)],
            )
            for lane in range(lanes)
        ]

    def wait(copies):
        for copy in copies:
            copy.wait()

    leaving = []
    for expert in range(count):
        arriving = [load(expert, 0)]
        if expert == 0:
            rows = {1: [start(inputs[1], blocks_ref.at[1])]}
        arriving.append(load(expert, 1))
        if expert == 0:
            slopes = {1: [start(inputs[3], grads_ref.at[1])]}
        arriving.append(load(expert, 2))
        if expert == 0:
            rows[0] = [start(inputs[0], blocks_ref.at[0])]
            slopes[0] = [start(inputs[2], grads_ref.at[0])]
        for side, out_ref in ((1, other_ref), (0, mine_ref)):
            block_ref, grad_ref = blocks_ref.at[side], grads_ref.at[side]
            if expert == 0:
                wait(rows[side])
            if side == 1:
                wait(arriving[0])
            number = expert_ref[expert]
            scale = gate_column(block_ref, width, number)
            block = block_ref[:, :width]
            gate = dot(block, held_ref[0], 1, 1)
            if side == 1:
                wait(arriving[1])
            up = dot(block, held_ref[1], 1, 1)
            if expert == 0:
                wait(slopes[side])
            if side == 1:
                wait(arriving[2])
            grad_raw = dot(grad_ref[...], held_ref[2], 1, 1)
            bent, slope = gelu_parts(gate)
            active = bent * up
            row_sum = jnp.sum(grad_raw * active, axis=1, keepdims=True)
            grad_active = grad_raw * scale
            grad_gate = (grad_active * up * slope).astype(BF)
            grad_up = (grad_active * bent).astype(BF)
            weighted = (active * scale).astype(BF)
            hidden_ref[side, 0] = grad_gate
            hidden_ref[side, 1] = grad_up
            hidden_ref[side, 2] = weighted
            term = dot(grad_gate, held_ref[0], 1, 0) + dot(grad_up, held_ref[1], 1, 0)
            hit = lax.broadcasted_iota(jnp.int32, (block.shape[0], 128), 1) == number
            gates = jnp.where(hit, row_sum, 0.0)
            ahead = dot(weighted, held_ref[2], 1, 0) if forward else None
            if count == 1:
                out_ref[:, :width] = term.astype(out_ref.dtype)
                out_ref[:, width:] = gates.astype(out_ref.dtype)
                if forward:
                    terms_refs[side][...] = ahead.astype(terms_refs[side].dtype)
            else:
                if expert > 0:
                    term = term + out_ref[:, :width].astype(F32)
                    gates = gates + out_ref[:, width:].astype(F32)
                out_ref[:, :width] = term.astype(out_ref.dtype)
                out_ref[:, width:] = gates.astype(out_ref.dtype)
                if forward:
                    if expert > 0:
                        ahead = ahead + terms_refs[side][...].astype(F32)
                    terms_refs[side][...] = ahead.astype(terms_refs[side].dtype)
            if expert == count - 1:
                leaving.append(start(out_ref, outs[side]))
                if forward:
                    leaving.append(start(terms_refs[side], outs[3 + side]))
        if expert > 0:
            wait(weights_leaving)
        weights_leaving = []
        for index in (2, 0, 1):
            total = None
            for side in (0, 1):
                right = grads_ref[side] if index == 2 else blocks_ref[side, :, :width]
                term = dot(hidden_ref[side, index], right, 0, 0)
                total = term if total is None else total + term
            weight_ref[index] = total.astype(BF)
            weights_leaving += [
                start(
                    weight_ref.at[index, pl.ds(lane * units, units)],
                    outs[2].at[lane, expert, index],
                )
                for lane in range(lanes)
            ]
    wait(leaving)
    wait(weights_leaving)


def row_parts(rows):
    parts = 1
    while rows % parts or rows // parts > ROWS_HELD:
        parts += 1
    return parts


def by_parts(call, *sides):
    rows = sides[0][0].shape[0]
    size = rows // row_parts(rows)
    return [
        call(*[[member[at : at + size] for member in side] for side in sides])
        for at in range(0, rows, size)
    ]


def experts_back(blocks, grads, weights, plan, forward):
    found = by_parts(
        lambda some, slopes: experts_back_part(some, slopes, weights, plan, forward), blocks, grads
    )
    if len(found) == 1:
        return found[0]
    found = list(zip(*found))
    return [
        sum(member.astype(F32) for member in members).astype(BF)
        if index == 2
        else jnp.concatenate(members, axis=0)
        for index, members in enumerate(found)
    ]


def experts_back_part(blocks, grads, weights, plan, forward, events=()):
    lanes, count, _, units, width = weights.shape
    rows = blocks[0].shape[0]
    hidden = lanes * units
    out_shape = [
        jax.ShapeDtypeStruct((rows, width + 128), F32),
        jax.ShapeDtypeStruct((rows, width + 128), BF),
        jax.ShapeDtypeStruct(weights.shape, BF),
    ]
    scratch = [
        pltpu.VMEM((2, rows, width + 128), BF),
        pltpu.VMEM((2, rows, width), BF),
        pltpu.VMEM((3, hidden, width), BF),
        pltpu.VMEM((rows, width + 128), F32),
        pltpu.VMEM((rows, width + 128), BF),
        pltpu.VMEM((2, 3, rows, hidden), BF),
        pltpu.VMEM((3, hidden, width), BF),
    ]
    if forward:
        for dtype in (F32, BF):
            out_shape.append(jax.ShapeDtypeStruct((rows, width), dtype))
            scratch.append(pltpu.VMEM((rows, width), dtype))
    scratch.append(pltpu.SemaphoreType.DMA((8 + 6 * lanes * count,)))
    anywhere = pl.BlockSpec(memory_space=pl.ANY)
    return pl.pallas_call(
        functools.partial(experts_back_kernel, forward, len(events)),
        in_specs=[pl.BlockSpec(memory_space=pltpu.SMEM)] + [anywhere] * (5 + len(events)),
        out_specs=[anywhere] * len(out_shape),
        out_shape=out_shape,
        scratch_shapes=scratch,
        compiler_params=kernel_params(0),
        name="experts_back",
    )(plan["experts"], *blocks, *grads, weights, *events)


def layer_backward(grad_out, grad_blocks, kept, weights, plan, forward, background):
    stream, attention_kept, middle, moe_in, blocks, chosen, within = kept
    mine, other, expert_grads, *terms = experts_back(
        blocks, grad_blocks, weights["experts"], plan, forward
    )
    events = background(mine)
    if events:
        other = tie(other, events[0], events[2])
    grad_moe = rows_reduce(mine, other, stream.shape[0])
    width = middle.shape[1]
    grad_gate = grad_moe[:, width : width + within.shape[1]] * within
    grad_moe = grad_moe[:, :width]
    gates = gate_values(dot(moe_in, weights["router"], 1, 0), chosen)
    grad_logits = gates * (grad_gate - jnp.sum(gates * grad_gate, axis=-1, keepdims=True))
    grad_logits = grad_logits.astype(BF)
    grad_moe = grad_moe + dot(grad_logits, weights["router"], 1, 1)
    grad_router = dot(moe_in, grad_logits, 0, 0)
    _, pull = jax.vjp(norm_rows, middle, weights["gains"][1])
    grad_middle, grad_gain_moe = pull(grad_moe)
    grad_middle = grad_middle + grad_out
    grad_stream, grad_q, grad_o, grad_kv, grad_gain = attention_backward(
        grad_middle, stream, attention_kept, weights, plan, events
    )
    extras = jnp.concatenate([grad_router, grad_gain[:, None], grad_gain_moe[:, None]], axis=1)
    grad_small = jnp.concatenate([grad_kv, pad_columns(extras)], axis=1)
    return grad_stream, (grad_q, grad_o, grad_small, expert_grads), terms


def pad_columns(values, columns=128):
    return jnp.pad(values, ((0, 0), (0, columns - values.shape[1])))


def holder():
    return (lax.axis_index("tensor") // 2) == lax.axis_index("section")


def head_columns(kv_weight, head):
    half = kv_weight.shape[1] // 2
    return jnp.concatenate(
        [kv_weight[:, head * HD : (head + 1) * HD], kv_weight[:, half + head * HD : half + (head + 1) * HD]],
        axis=1,
    )


def to_holders(own):
    lanes = lax.axis_size("tensor")
    pairs = [(t, lanes + t) for t in range(lanes // 2, lanes)]
    pairs += [(lanes + t, t) for t in range(lanes // 2)]
    moved = lax.ppermute(own, ("section", "tensor"), pairs)
    leading = lax.axis_index("section") == 0
    return jnp.where(leading, own, moved), jnp.where(leading, moved, own)


def from_holders(first, second):
    lanes = lax.axis_size("tensor")
    pairs = [(lanes + t, t) for t in range(lanes // 2, lanes)]
    pairs += [(t, lanes + t) for t in range(lanes // 2)]
    leading = lax.axis_index("section") == 0
    moved = lax.ppermute(jnp.where(leading, second, first), ("section", "tensor"), pairs)
    return jnp.where(holder(), jnp.where(leading, first, second), moved)


def reduce_small(parts, until=None):
    lanes = lax.axis_size("tensor")
    return lanes_reduce(parts.reshape(lanes, -1, parts.shape[1]), until)


def panels(grads):
    pieces = lax.axis_size("dp")
    return to_staged(grads.astype(BF).reshape(pieces, -1, grads.shape[1]))


def per_device(edge_in, routes, q_weight, o_weight, kv_weight, router, gains, w_in, w_out):
    section = lax.axis_index("section")
    leading = section == 0
    lanes = lax.axis_size("tensor")
    pieces = lax.axis_size("dp")
    rows = edge_in.shape[2]
    piece_rows = rows * lanes
    prompt_dev = PROMPT // pieces
    local, units, width = w_out.shape[1:]
    experts = local * pieces
    top = routes.shape[3]
    capacity = lanes * (
        (9 * piece_rows * top + 8 * experts * lanes - 1) // (8 * experts * lanes)
    )

    edge_kept = lax.dynamic_index_in_dim(edge_in[0], section, 0, keepdims=False)
    edge_got = section_swap(lax.dynamic_index_in_dim(edge_in[0], 1 - section, 0, keepdims=False))
    stream = jnp.where(leading, edge_kept, edge_got).astype(F32)
    cotangent = jnp.where(leading, edge_got, edge_kept)
    route_kept = lax.dynamic_index_in_dim(routes[0], section, 0, keepdims=False)
    route_got = section_swap(lax.dynamic_index_in_dim(routes[0], 1 - section, 0, keepdims=False))
    route_first = jnp.where(leading, route_kept, route_got)
    route_second = jnp.where(leading, route_got, route_kept)

    share = local // 2
    pack = jnp.stack([w_in[0, :, 0], w_in[0, :, 1], w_out[0]], axis=1)
    pack_kept = lax.dynamic_slice_in_dim(pack, section * share, share, 0)
    pack_got = section_swap(lax.dynamic_slice_in_dim(pack, (1 - section) * share, share, 0))
    pack_first = jnp.where(leading, pack_kept, pack_got)
    pack_second = jnp.where(leading, pack_got, pack_kept)
    experts_first = lax.all_gather(pack_first, "tensor", axis=0, tiled=False)

    masks = [route_masks(ids, experts, capacity) for ids in (route_first, route_second)]
    masks = [
        [
            lax.dynamic_slice_in_dim(member, lax.axis_index("tensor") * rows, rows, 0).astype(F32)
            for member in pair
        ]
        for pair in masks
    ]
    squares = to_holders(jnp.stack([q_weight[0], o_weight[0]]))
    extras = pad_columns(jnp.concatenate([router[0], gains[0].T], axis=1))
    heads = [jnp.concatenate([head_columns(kv_weight[0], h), extras], axis=1) for h in range(2)]
    small_kept = jnp.where(leading, heads[0], heads[1])
    small_got = section_swap(jnp.where(leading, heads[1], heads[0]))
    small_first = jnp.where(leading, small_kept, small_got)
    small_second = jnp.where(leading, small_got, small_kept)
    small_cols = small_kept.shape[1]
    query_cols = QH // 2 * HD
    panel = jnp.concatenate([holders_gather(squares[0][0]), lanes_gather(small_first, 0)], axis=1)
    qkv_first = from_staged(staged_gather(tie(panel, pack_first)))

    def layer_weights(layer, qkv):
        extras = qkv[:, query_cols + 2 * HD :]
        return {
            "qkv": qkv,
            "router": extras[:, :experts],
            "gains": extras[:, experts : experts + 2].T.astype(F32),
        }

    piece_index = lax.axis_index("dp")
    tables = rope_tables(own_places(rows, prompt_dev))
    plan = {
        "prompt_dev": prompt_dev,
        "rope": tables,
        "rope_both": [jnp.concatenate([table, table], axis=0) for table in tables],
        "bias": jnp.where(allowed_pairs(rows, piece_rows, prompt_dev), 0.0, NEGATIVE),
        "experts": piece_index * local + section * share + jnp.arange(share, dtype=jnp.int32),
    }
    def experts_rows(layer, middle):
        moe_in = norm_rows(middle, weights[layer]["gains"][1]).astype(BF)
        chosen, within = masks[layer]
        gates = gate_values(dot(moe_in, weights[layer]["router"], 1, 0), chosen) * within
        moe_rows = jnp.concatenate([moe_in, pad_columns(gates.astype(BF))], axis=1)
        return moe_in, rows_gather(moe_rows)

    weights = [layer_weights(0, qkv_first), None]
    weights[0]["experts"] = experts_first

    def fetch_first(normed, piece, prompt):
        o_first = holders_gather(tie(squares[0][1], panel), normed)
        return from_staged(staged_gather(o_first, (piece, prompt)))

    middle_first, attention_first = attention_forward(
        stream, weights[0], plan, (), fetch_first
    )
    prompt, attended = attention_first[2], attention_first[4]
    small_second = lanes_gather(tie(small_second, prompt), 0, attended)
    moe_first, blocks_first = experts_rows(0, middle_first)
    q_second = holders_gather(tie(squares[1][0], attended), blocks_first[0])
    mine, other = experts_forward(blocks_first, experts_first, plan)
    result = middle_first + rows_reduce(mine, other, rows)
    hidden = result.astype(BF).astype(F32)
    panel = jnp.concatenate([q_second, small_second], axis=1)
    qkv_second = from_staged(staged_gather(panel, (other, result)))
    o_second = holders_gather(tie(squares[1][1], blocks_first[0]), result)

    grad_blocks = rows_gather(cotangent)
    weights[1] = layer_weights(1, qkv_second)
    weights[1]["experts"] = lax.all_gather(
        tie(pack_second, blocks_first[0]), "tensor", axis=0, tiled=False
    )

    def fetch_second(normed, piece, prompt):
        return from_staged(staged_gather(tie(o_second, normed), (piece, prompt)))

    middle_second, attention_second = attention_forward(
        hidden, weights[1], plan, (), fetch_second
    )
    moe_second, blocks_second = experts_rows(1, middle_second)

    kept = (hidden, attention_second, middle_second, moe_second, blocks_second, *masks[1])
    grad_stream, grads, terms = layer_backward(
        cotangent.astype(F32), grad_blocks, kept, weights[1], plan, True, lambda mine: ()
    )
    q_second, o_second, small_second, experts_second = grads
    half = q_second.shape[0]
    grad_out = grad_stream.astype(BF)
    grad_blocks = rows_gather(grad_out)
    second = []

    def beside_first(mine):
        squares = tie(jnp.concatenate([q_second, o_second], axis=0), grad_blocks[0])
        second.append(holders_reduce(squares, mine))
        second.append(reduce_stage(panels(small_second), dp_bits() - 1, mine))
        total = terms[0] + section_swap(terms[1]).astype(F32)
        total = tie(total, grad_blocks[0]).reshape(-1, rows, width)
        second.append(reduce_stage(total, dp_bits() - 1, mine))
        return second

    kept = (stream, attention_first, middle_first, moe_first, blocks_first, *masks[0])
    grad_stream, grads, _ = layer_backward(
        grad_out.astype(F32), grad_blocks, kept, weights[0], plan, False, beside_first
    )
    square_second, small_second, result = second
    small_second = reduce_rest(small_second)
    result = middle_second + reduce_rest(result)

    edge_kept = jnp.where(leading, grad_stream, result)
    edge_got = section_swap(jnp.where(leading, result, grad_stream))
    edge_out = jnp.where(
        leading, jnp.stack([edge_kept, edge_got]), jnp.stack([edge_got, edge_kept])
    )

    q_first, o_first, small_first, experts_first = grads
    square_first = holders_reduce(jnp.concatenate([q_first, o_first], axis=0))
    small_first = staged_reduce(panels(small_first))
    smalls = reduce_small(jnp.concatenate([small_first, small_second], axis=1))
    small_first, small_second = smalls[:, :small_cols], smalls[:, small_cols:]
    both = from_holders(square_first, square_second)
    grad_q, grad_o = both[:half], both[half:]
    small_kept = jnp.where(leading, small_first, small_second)
    small_got = section_swap(jnp.where(leading, small_second, small_first))
    key_values = jnp.where(
        leading,
        jnp.stack([small_kept[:, : 2 * HD], small_got[:, : 2 * HD]]),
        jnp.stack([small_got[:, : 2 * HD], small_kept[:, : 2 * HD]]),
    )
    grad_kv = jnp.concatenate(
        [key_values[0, :, :HD], key_values[1, :, :HD], key_values[0, :, HD:], key_values[1, :, HD:]],
        axis=1,
    )
    extras = small_kept[:, 2 * HD :] + small_got[:, 2 * HD :]

    summed = [
        lax.psum_scatter(member, "tensor", scatter_dimension=0, tiled=False)
        for member in (experts_first, experts_second)
    ]
    second_got = section_send(summed[1], 0)
    first_got = section_send(summed[0], 1)
    grad_experts = jnp.concatenate(
        [jnp.where(leading, summed[0], second_got), jnp.where(leading, first_got, summed[1])],
        axis=0,
    ).astype(F32)
    return (
        edge_out[None],
        grad_q[None],
        grad_o[None],
        grad_kv[None],
        extras[None, :, :experts],
        extras[:, experts : experts + 2].T[None],
        grad_experts[None, :, :2],
        grad_experts[None, :, 2],
    )


def solution(mesh):
    placed = (
        P("section", None, ("dp", "tensor"), None),
        P("section", None, "dp", None),
        P("section", "dp", "tensor"),
        P("section", "dp", "tensor"),
        P("section", ("dp", "tensor"), None),
        P("section", ("dp", "tensor"), None),
        P("section", None, ("dp", "tensor")),
        P("section", "dp", None, "tensor", None),
        P("section", "dp", "tensor", None),
    )
    return jax.shard_map(
        per_device,
        mesh=mesh,
        in_specs=placed,
        out_specs=(placed[0],) + placed[2:],
        check_vma=False,
    )
```

```python
import functools
import math

import jax
import jax.numpy as jnp
from jax import lax
from jax.experimental import pallas as pl
from jax.experimental.pallas import tpu as pltpu
from jax.sharding import PartitionSpec as P

QH = 12
KVH = 2
HD = 128
PROMPT = 1024
CONT = 256

EPSILON = 1e-06
NEGATIVE = -1e30
ROPE_BASE = 10000.0
BF = jnp.bfloat16
F32 = jnp.float32
VMEM_BYTES = 56 * 1024 * 1024
ROWS_HELD = 512
GELU_SCALE = math.sqrt(2.0 / math.pi)
GELU_CUBE = 0.044715


def dot(left, right, left_axis, right_axis):
    return lax.dot_general(
        left, right, (((left_axis,), (right_axis,)), ((), ())), preferred_element_type=F32
    )


def norm_rows(values, gain):
    return values * lax.rsqrt(jnp.mean(values * values, axis=-1, keepdims=True) + EPSILON) * gain


def gelu_parts(values):
    square = values * values
    bent = jnp.tanh(GELU_SCALE * values * (1.0 + GELU_CUBE * square))
    half = 0.5 * (1.0 + bent)
    slope = half + 0.5 * values * (1.0 - bent * bent) * (
        GELU_SCALE * (1.0 + 3.0 * GELU_CUBE * square)
    )
    return values * half, slope


def kernel_params(axes):
    return pltpu.CompilerParams(
        vmem_limit_bytes=VMEM_BYTES,
        dimension_semantics=("arbitrary",) * axes if axes else None,
    )


def tree_swap(values, axis, pairs):
    return jax.tree.map(lambda v: lax.ppermute(v, axis, pairs), values)


def section_swap(values):
    return tree_swap(values, "section", [(0, 1), (1, 0)])


def section_send(values, source):
    return tree_swap(values, "section", [(source, 1 - source)])


def dp_bits():
    return lax.axis_size("dp").bit_length() - 1


def stage_bit(section, stage):
    return stage if section == 0 else dp_bits() - 1 - stage


def stage_swap(values, stage):
    count = lax.axis_size("dp")
    pairs = [
        (s * count + d, s * count + (d ^ (1 << stage_bit(s, stage))))
        for s in range(2)
        for d in range(count)
    ]
    return lax.ppermute(values, ("section", "dp"), pairs)


def stage_origin(position):
    origins = []
    for section in range(2):
        moved = jnp.int32(0)
        for stage in range(dp_bits()):
            moved = moved | ((position >> stage) & 1) << stage_bit(section, stage)
        origins.append(moved)
    return lax.axis_index("dp") ^ jnp.where(lax.axis_index("section") == 0, *origins)


def stage_position(origin):
    moved = origin ^ lax.axis_index("dp")
    positions = []
    for section in range(2):
        position = jnp.int32(0)
        for stage in range(dp_bits()):
            position = position | ((moved >> stage_bit(section, stage)) & 1) << stage
        positions.append(position)
    return jnp.where(lax.axis_index("section") == 0, *positions)


def stage_join(block, stage, until):
    moved = stage_swap(block, stage)
    if until is not None:
        moved = tie(moved, *until) if isinstance(until, tuple) else tie(moved, until)
    return jnp.concatenate([block, moved], axis=0)


def staged_gather(block, until=()):
    block = block[None]
    for stage in range(dp_bits()):
        block = stage_join(block, stage, until[min(stage, len(until) - 1)] if until else None)
    return block


def staged_reduce(parts, since=(), until=()):
    for turn, stage in enumerate(reversed(range(dp_bits()))):
        half = parts.shape[0] // 2
        leaving = parts[half:].astype(BF)
        if since and since[min(turn, len(since) - 1)] is not None:
            leaving = tie(leaving, since[min(turn, len(since) - 1)])
        arrived = stage_swap(leaving, stage)
        if until and until[min(turn, len(until) - 1)] is not None:
            arrived = tie(arrived, until[min(turn, len(until) - 1)])
        parts = parts[:half].astype(F32) + arrived.astype(F32)
    return parts[0].astype(F32)


def reduce_stage(parts, stage, until):
    half = parts.shape[0] // 2
    arrived = tie(stage_swap(parts[half:].astype(BF), stage), until)
    return parts[:half].astype(F32) + arrived.astype(F32)


def reduce_rest(parts):
    for stage in reversed(range(dp_bits() - 1)):
        half = parts.shape[0] // 2
        arrived = stage_swap(parts[half:].astype(BF), stage)
        parts = parts[:half] + arrived.astype(F32)
    return parts[0]


def to_staged(blocks):
    return jnp.concatenate(
        [
            lax.dynamic_slice_in_dim(blocks, stage_origin(jnp.int32(p)), 1, 0)
            for p in range(blocks.shape[0])
        ],
        axis=0,
    )


def from_staged(blocks):
    blocks = jnp.concatenate(
        [
            lax.dynamic_slice_in_dim(blocks, stage_position(jnp.int32(d)), 1, 0)
            for d in range(blocks.shape[0])
        ],
        axis=0,
    )
    return blocks.reshape(-1, blocks.shape[-1])


def mirrored():
    here = lax.axis_index("tensor")
    return jnp.where(lax.axis_index("section") == 0, here, lax.axis_size("tensor") - 1 - here)


def mirrored_send(values, pairs):
    lanes = lax.axis_size("tensor")
    routes = [(a, b) for a, b in pairs]
    routes += [(2 * lanes - 1 - a, 2 * lanes - 1 - b) for a, b in pairs]
    return lax.ppermute(values, ("section", "tensor"), routes)


def holders_gather(block, until=None):
    place = mirrored()
    near = mirrored_send(block, [(0, 1), (1, 2)])
    far = mirrored_send(block, [(0, 2), (1, 3)])
    last = mirrored_send(block, [(0, 3), (1, 0)])
    if until is not None:
        near, far, last = tie((near, far, last), until)
    outer = jnp.where(
        place == 0, block, jnp.where(place == 1, near, jnp.where(place == 2, far, last))
    )
    inner = jnp.where(
        place == 0, last, jnp.where(place == 1, block, jnp.where(place == 2, near, far))
    )
    leading = lax.axis_index("section") == 0
    return jnp.concatenate(
        [jnp.where(leading, outer, inner), jnp.where(leading, inner, outer)], axis=1
    )


def holders_reduce(parts, until=None):
    place = mirrored()
    leading = lax.axis_index("section") == 0
    cols = parts.shape[1] // 2
    outer = jnp.where(leading, parts[:, :cols], parts[:, cols:])
    inner = jnp.where(leading, parts[:, cols:], parts[:, :cols])
    total = jnp.where(place == 0, outer, inner)
    outer, inner = outer.astype(BF), inner.astype(BF)
    near = mirrored_send(jnp.where(place == 1, outer, inner), [(1, 0), (2, 1)])
    far = mirrored_send(jnp.where(place == 2, outer, inner), [(2, 0), (3, 1)])
    last = mirrored_send(jnp.where(place == 3, outer, inner), [(3, 0), (0, 1)])
    if until is not None:
        near, far, last = tie((near, far, last), until)
    return total + near.astype(F32) + far.astype(F32) + last.astype(F32)


def lanes_gather(block, axis, until=None):
    lanes = lax.axis_size("tensor")
    here = lax.axis_index("tensor")
    blocks = [block]
    for apart in range(1, lanes):
        blocks.append(
            lax.ppermute(block, "tensor", [(i, (i - apart) % lanes) for i in range(lanes)])
        )
    if until is not None:
        blocks[1:] = tie(blocks[1:], until)
    size = block.shape[axis]
    return lax.dynamic_slice_in_dim(
        jnp.concatenate(blocks + blocks[: lanes - 1], axis=axis),
        jnp.where(here == 0, 0, lanes - here) * size,
        lanes * size,
        axis,
    )


def lanes_reduce(parts, until=None):
    lanes = lax.axis_size("tensor")
    here = lax.axis_index("tensor")
    total = lax.dynamic_index_in_dim(parts, here, 0, keepdims=False)
    for apart in range(1, lanes):
        term = lax.dynamic_index_in_dim(parts, (here + apart) % lanes, 0, keepdims=False)
        pairs = [(i, (i + apart) % lanes) for i in range(lanes)]
        arrived = lax.ppermute(term.astype(BF), "tensor", pairs)
        if until is not None:
            arrived = tie(arrived, until)
        total = total + arrived.astype(F32)
    return total


def tie(values, *events):
    probe = sum(event[(0,) * event.ndim].astype(F32) for event in events)
    return jax.tree.map(lambda v: jnp.where(probe != probe, jnp.zeros((), v.dtype), v), values)


def rows_gather(block, until=()):
    mine = staged_gather(block, until).reshape(-1, block.shape[1])
    return mine, section_swap(mine)


def rows_reduce(mine, other, rows, until=None):
    arrived = section_swap(other.astype(BF))
    if until is not None:
        arrived = tie(arrived, until[0])
    total = mine.astype(F32) + arrived.astype(F32)
    return staged_reduce(
        total.reshape(-1, rows, total.shape[1]), until=until[1:] if until is not None else ()
    )


def rope_tables(places):
    half = HD // 2
    frequency = jnp.exp(jnp.arange(half, dtype=F32) * (-math.log(ROPE_BASE) / half))
    angles = places.astype(F32)[:, None] * frequency[None, :]
    cosine, sine = jnp.cos(angles), jnp.sin(angles)
    return (
        jnp.concatenate([cosine, cosine], axis=1),
        jnp.concatenate([-sine, sine], axis=1),
    )


def rotate(values, tables, sign):
    half = HD // 2
    turned = jnp.concatenate([values[:, half:], values[:, :half]], axis=1)
    return values * tables[0] + turned * (sign * tables[1])


def key_value_gather(key_value, prompt_dev):
    piece = lanes_gather(key_value, 1)
    return staged_gather(piece[:, :prompt_dev]), piece


def lanes_parts(piece, rows):
    batches, _, width = piece.shape
    return piece.reshape(batches, -1, rows, width).transpose(1, 0, 2, 3)


def allowed_pairs(rows, piece_rows, prompt_dev):
    piece_index = lax.axis_index("dp")
    ordinal = lax.axis_index("tensor") * rows + jnp.arange(rows, dtype=jnp.int32)
    columns = jnp.arange(PROMPT + piece_rows - prompt_dev, dtype=jnp.int32)
    key_place = stage_origin(columns // prompt_dev) * prompt_dev + columns % prompt_dev
    query_prompt = ordinal < prompt_dev
    query_place = piece_index * prompt_dev + ordinal
    query_cont = (ordinal - prompt_dev) // CONT
    query_step = (ordinal - prompt_dev) % CONT
    local_col = columns - PROMPT
    prompt_part = jnp.logical_or(
        jnp.logical_not(query_prompt)[:, None], key_place[None, :] <= query_place[:, None]
    )
    cont_part = jnp.logical_and(
        jnp.logical_not(query_prompt)[:, None],
        jnp.logical_and(
            local_col[None, :] // CONT == query_cont[:, None],
            local_col[None, :] % CONT <= query_step[:, None],
        ),
    )
    return jnp.where((columns < PROMPT)[None, :], prompt_part, cont_part)


def own_places(rows, prompt_dev):
    piece_index = lax.axis_index("dp")
    ordinal = lax.axis_index("tensor") * rows + jnp.arange(rows, dtype=jnp.int32)
    return jnp.where(
        ordinal < prompt_dev,
        piece_index * prompt_dev + ordinal,
        PROMPT + (ordinal - prompt_dev) % CONT,
    )


def with_other(values):
    return jnp.concatenate([values, section_swap(values)], axis=0)


def sum_with_other(values):
    rows = values.shape[0] // 2
    return values[:rows] + section_swap(values[rows:].astype(BF)).astype(F32)


def attend_kernel(query_ref, prompt_ref, piece_ref, bias_ref, cos_ref, sin_ref, *refs):
    out_ref, queries_ref, rows_ref, scores_ref, probs_ref = refs[-5:]
    rows, cols = query_ref.shape
    heads = cols // HD
    prompt_dev = prompt_ref.shape[2]
    seen = rows_ref.shape[0]
    rows_ref[:PROMPT] = prompt_ref[...].reshape(PROMPT, 2 * HD)
    rows_ref[PROMPT:] = piece_ref[0, prompt_dev:]
    cosine, sine = cos_ref[...], sin_ref[...]
    queries = []
    for head in range(heads):
        part = query_ref[:, head * HD : (head + 1) * HD]
        part = part * cosine + pltpu.roll(part, HD // 2, 1) * sine
        part = part.astype(BF)
        queries_ref[:, head * HD : (head + 1) * HD] = part
        queries.append(part)
    keys, values = rows_ref[:, :HD], rows_ref[:, HD:]
    scores_ref[...] = dot(jnp.concatenate(queries, axis=0), keys, 1, 1)
    step = rows

    def softmax(index, carry):
        at = pl.multiple_of(index * step, step)
        bias = bias_ref[...]
        scores = scores_ref[pl.ds(at, step), :] * (1.0 / math.sqrt(HD)) + bias
        exponent = jnp.exp(scores - jnp.max(scores, axis=1, keepdims=True))
        total = jnp.sum(exponent, axis=1, keepdims=True)
        probs_ref[pl.ds(at, step), :] = (exponent / total).astype(BF)
        return carry

    lax.fori_loop(0, heads, softmax, 0, unroll=2)
    attended = dot(probs_ref[...], values, 1, 0).astype(BF)
    for head in range(heads):
        out_ref[:, head * HD : (head + 1) * HD] = attended[head * rows : (head + 1) * rows]


def attend(projected, prompt, piece, plan, events):
    rows = projected.shape[0] // 2
    cols = QH // 2 * HD
    pieces, _, prompt_dev, width = prompt.shape
    seen = PROMPT + piece.shape[1] - prompt_dev
    shape = jax.ShapeDtypeStruct((2 * rows, cols), BF)
    block = pl.BlockSpec((rows, cols), lambda b: (b, 0))
    table = pl.BlockSpec((rows, HD), lambda b: (0, 0))
    heads = cols // HD
    return pl.pallas_call(
        attend_kernel,
        grid=(2,),
        in_specs=[
            block,
            pl.BlockSpec((pieces, 1, prompt_dev, width), lambda b: (0, b, 0, 0)),
            pl.BlockSpec((1,) + piece.shape[1:], lambda b: (b, 0, 0)),
            pl.BlockSpec((rows, seen), lambda b: (0, 0)),
            table,
            table,
        ]
        + [pl.BlockSpec(memory_space=pl.ANY)] * len(events),
        out_specs=[block, block],
        out_shape=[shape, shape],
        scratch_shapes=[
            pltpu.VMEM((seen, width), BF),
            pltpu.VMEM((heads * rows, seen), F32),
            pltpu.VMEM((heads * rows, seen), BF),
        ],
        compiler_params=kernel_params(1),
        name="attend",
    )(projected, prompt, piece, plan["bias"], *plan["rope"], *events)


def attend_back_kernel(query_ref, grad_ref, prompt_ref, piece_ref, bias_ref, cos_ref, sin_ref, *refs):
    out_ref, prompt_out, piece_out, rows_ref, scores_ref, slopes_ref, probs_ref, dscores_ref = refs[-8:]
    rows, cols = query_ref.shape
    heads = cols // HD
    prompt_dev = prompt_ref.shape[2]
    pieces = prompt_ref.shape[0]
    scale = 1.0 / math.sqrt(HD)
    rows_ref[:PROMPT] = prompt_ref[...].reshape(PROMPT, 2 * HD)
    rows_ref[PROMPT:] = piece_ref[0, prompt_dev:]
    keys, values = rows_ref[:, :HD], rows_ref[:, HD:]
    split = [(head * HD, (head + 1) * HD) for head in range(heads)]
    queries = jnp.concatenate([query_ref[:, a:b] for a, b in split], axis=0)
    grads = jnp.concatenate([grad_ref[:, a:b] for a, b in split], axis=0)
    scores_ref[...] = dot(queries, keys, 1, 1)
    slopes_ref[...] = dot(grads, values, 1, 1)
    step = rows

    def softmax(index, carry):
        at = pl.multiple_of(index * step, step)
        bias = bias_ref[...]
        scores = scores_ref[pl.ds(at, step), :] * scale + bias
        exponent = jnp.exp(scores - jnp.max(scores, axis=1, keepdims=True))
        probs = exponent / jnp.sum(exponent, axis=1, keepdims=True)
        slopes = slopes_ref[pl.ds(at, step), :]
        delta = jnp.sum(probs * slopes, axis=1, keepdims=True)
        probs_ref[pl.ds(at, step), :] = probs.astype(BF)
        dscores_ref[pl.ds(at, step), :] = (probs * (slopes - delta)).astype(BF)
        return carry

    lax.fori_loop(0, heads, softmax, 0, unroll=2)
    dscores = dscores_ref[...]
    grad_query = dot(dscores, keys, 1, 0) * scale
    cosine, sine = cos_ref[...], sin_ref[...]
    for head, (a, b) in enumerate(split):
        part = grad_query[head * rows : (head + 1) * rows]
        out_ref[:, a:b] = (part * cosine - pltpu.roll(part, HD // 2, 1) * sine).astype(BF)
    grad_keys = dot(dscores, queries, 0, 0) * scale
    grad_values = dot(probs_ref[...], grads, 0, 0)
    prompt_out[:, 0, :, :HD] = grad_keys[:PROMPT].reshape(pieces, prompt_dev, HD)
    prompt_out[:, 0, :, HD:] = grad_values[:PROMPT].reshape(pieces, prompt_dev, HD)
    piece_out[0, :, :HD] = grad_keys[PROMPT:]
    piece_out[0, :, HD:] = grad_values[PROMPT:]


def attend_back(queries, grad_attended, prompt, piece, plan, events):
    rows, cols = queries.shape[0] // 2, queries.shape[1]
    pieces, _, prompt_dev, width = prompt.shape
    own = piece.shape[1] - prompt_dev
    seen = PROMPT + own
    block = pl.BlockSpec((rows, cols), lambda b: (b, 0))
    table = pl.BlockSpec((rows, HD), lambda b: (0, 0))
    prompt_block = pl.BlockSpec((pieces, 1, prompt_dev, width), lambda b: (0, b, 0, 0))
    heads = cols // HD
    return pl.pallas_call(
        attend_back_kernel,
        grid=(2,),
        in_specs=[
            block,
            block,
            prompt_block,
            pl.BlockSpec((1,) + piece.shape[1:], lambda b: (b, 0, 0)),
            pl.BlockSpec((rows, seen), lambda b: (0, 0)),
            table,
            table,
        ]
        + [pl.BlockSpec(memory_space=pl.ANY)] * len(events),
        out_specs=[block, prompt_block, pl.BlockSpec((1, own, width), lambda b: (b, 0, 0))],
        out_shape=[
            jax.ShapeDtypeStruct(queries.shape, BF),
            jax.ShapeDtypeStruct(prompt.shape, F32),
            jax.ShapeDtypeStruct((2, own, width), F32),
        ],
        scratch_shapes=[
            pltpu.VMEM((seen, width), BF),
            pltpu.VMEM((heads * rows, seen), F32),
            pltpu.VMEM((heads * rows, seen), F32),
            pltpu.VMEM((heads * rows, seen), BF),
            pltpu.VMEM((heads * rows, seen), BF),
        ],
        compiler_params=kernel_params(1),
        name="attend_back",
    )(queries, grad_attended, prompt, piece, plan["bias"], *plan["rope"], *events)


def attention_forward(stream, weights, plan, events, fetch):
    rows = stream.shape[0]
    normed = norm_rows(stream, weights["gains"][0]).astype(BF)
    normed = with_other(normed)
    query_cols = QH // 2 * HD
    projected = dot(normed, weights["qkv"][:, query_cols : query_cols + 2 * HD], 1, 0)
    keys = rotate(projected[:, :HD], plan["rope_both"], 1.0)
    values = projected[:, HD:]
    projected = dot(normed, weights["qkv"][:, :query_cols], 1, 0)
    packed = jnp.concatenate([keys, values], axis=1).astype(BF).reshape(2, rows, 2 * HD)
    prompt, piece = key_value_gather(packed, plan["prompt_dev"])
    o_full = fetch(normed, piece, prompt)
    attended, queries = attend(projected, prompt, piece, plan, events)
    middle = stream + sum_with_other(dot(attended, o_full, 1, 1))
    return middle, (normed, queries, prompt, piece, attended, o_full)


def attention_backward(grad_middle, stream, kept, weights, plan, events):
    normed, queries, prompt, piece, attended, o_full = kept
    rows = stream.shape[0]
    grad_branch = with_other(grad_middle.astype(BF))
    grad_attended = dot(grad_branch, o_full, 1, 0).astype(BF)
    grad_o = panels(dot(grad_branch, attended, 0, 0))
    grad_query, grad_prompt, grad_piece = attend_back(
        queries, grad_attended, prompt, piece, plan, events
    )
    grad_prompt = staged_reduce(grad_prompt)
    grad_q = panels(dot(normed, grad_query, 0, 0))
    grads = lanes_reduce(lanes_parts(jnp.concatenate([grad_prompt, grad_piece], axis=1), rows))
    grad_o = staged_reduce(grad_o, (None, grad_prompt), (grad_query, grads))
    grads = grads.reshape(2 * rows, 2 * HD)
    grad_keys = rotate(grads[:, :HD], plan["rope_both"], -1.0)
    grad_kv = jnp.concatenate([grad_keys, grads[:, HD:]], axis=1).astype(BF)
    cols = grad_query.shape[1]
    grad_normed = dot(grad_query, weights["qkv"][:, :cols], 1, 1)
    grad_normed = grad_normed + dot(grad_kv, weights["qkv"][:, cols : cols + 2 * HD], 1, 1)
    grad_normed = sum_with_other(grad_normed)
    grad_q = staged_reduce(grad_q, (grad_prompt, None), (grads, grad_normed))
    grad_kv_weight = dot(normed, grad_kv, 0, 0)
    _, pull = jax.vjp(norm_rows, stream, weights["gains"][0])
    grad_stream, grad_gain = pull(grad_normed)
    return grad_stream + grad_middle, grad_q, grad_o, grad_kv_weight, grad_gain


def route_masks(route_ids, experts, capacity):
    ids = jnp.arange(experts, dtype=jnp.int32)
    chosen = jnp.sum((route_ids[:, :, None] == ids[None, None, :]).astype(F32), axis=1)
    rows = route_ids.shape[0]
    ordinal = jnp.arange(rows, dtype=jnp.int32)
    before = (ordinal[:, None] > ordinal[None, :]).astype(BF)
    slots = dot(before, chosen.astype(BF), 1, 0)
    kept = jnp.where(slots < capacity, chosen, 0.0)
    return chosen.astype(BF), kept.astype(BF)


def gate_values(logits, chosen):
    masked = jnp.where(chosen > 0, logits, NEGATIVE)
    exponent = jnp.exp(masked - jnp.max(masked, axis=-1, keepdims=True))
    return exponent / jnp.sum(exponent, axis=-1, keepdims=True)


def gate_column(block_ref, width, expert):
    columns = block_ref[:, width:].astype(F32)
    hit = lax.broadcasted_iota(jnp.int32, columns.shape, 1) == expert
    return jnp.sum(jnp.where(hit, columns, 0.0), axis=1, keepdims=True)


def experts_kernel(expert_ref, mine_ref, other_ref, weights_ref, mine_out, other_out, blocks_ref, held_ref, left_ref, right_ref, sems):
    lanes, count, three, units, _ = weights_ref.shape
    width = held_ref.shape[-1]
    used = iter(range(sems.shape[0]))

    def start(source, target):
        copy = pltpu.make_async_copy(source, target, sems.at[next(used)])
        copy.start()
        return copy

    rows = {}
    leaving = []
    for expert in range(count):
        arriving = []
        for index in range(three):
            arriving.append(
                [
                    start(
                        weights_ref.at[lane, expert, index],
                        held_ref.at[index, pl.ds(lane * units, units)],
                    )
                    for lane in range(lanes)
                ]
            )
            if expert == 0 and index < 2:
                rows[1 - index] = start((mine_ref, other_ref)[1 - index], blocks_ref.at[1 - index])
        for side, total_ref, out_ref in ((1, right_ref, other_out), (0, left_ref, mine_out)):
            block_ref = blocks_ref.at[side]
            if expert == 0:
                rows[side].wait()
            scale = gate_column(block_ref, width, expert_ref[expert])
            hidden = []
            for index in range(2):
                if side == 1:
                    for copy in arriving[index]:
                        copy.wait()
                hidden.append(dot(block_ref[:, :width], held_ref[index], 1, 1))
            weighted = (gelu_parts(hidden[0])[0] * hidden[1] * scale).astype(BF)
            if side == 1:
                for copy in arriving[2]:
                    copy.wait()
            term = dot(weighted, held_ref[2], 1, 0)
            if expert > 0:
                term = term + total_ref[...].astype(F32)
            total_ref[...] = term.astype(total_ref.dtype)
            if expert == count - 1:
                leaving.append(start(total_ref, out_ref))
    for copy in leaving:
        copy.wait()


def experts_forward(blocks, weights, plan):
    found = by_parts(lambda some: experts_forward_part(some, weights, plan), blocks)
    return [jnp.concatenate(members, axis=0) if len(members) > 1 else members[0] for members in zip(*found)]


def experts_forward_part(blocks, weights, plan):
    lanes, count, three, units, width = weights.shape
    rows = blocks[0].shape[0]
    anywhere = pl.BlockSpec(memory_space=pl.ANY)
    return pl.pallas_call(
        experts_kernel,
        in_specs=[pl.BlockSpec(memory_space=pltpu.SMEM)] + [anywhere] * 3,
        out_specs=[anywhere] * 2,
        out_shape=[
            jax.ShapeDtypeStruct((rows, width), BF),
            jax.ShapeDtypeStruct((rows, width), BF),
        ],
        scratch_shapes=[
            pltpu.VMEM((2, rows, width + 128), BF),
            pltpu.VMEM((three, lanes * units, width), BF),
            pltpu.VMEM((rows, width), BF),
            pltpu.VMEM((rows, width), BF),
            pltpu.SemaphoreType.DMA((4 + three * lanes * count,)),
        ],
        compiler_params=kernel_params(0),
        name="experts",
    )(plan["experts"], *blocks, weights)


def experts_back_kernel(forward, events, expert_ref, *refs):
    inputs, refs = refs[:5], refs[5 + events :]
    weights_ref = inputs[4]
    outs, refs = refs[: 5 if forward else 3], refs[5 if forward else 3 :]
    blocks_ref, grads_ref, held_ref, mine_ref, other_ref, hidden_ref, weight_ref = refs[:7]
    terms_refs, sems = refs[7:-1], refs[-1]
    lanes, count, _, units, _ = weights_ref.shape
    width = grads_ref.shape[-1]
    used = iter(range(sems.shape[0]))

    def start(source, target):
        copy = pltpu.make_async_copy(source, target, sems.at[next(used)])
        copy.start()
        return copy

    def load(expert, index):
        return [
            start(
                weights_ref.at[lane, expert, index],
                held_ref.at[index, pl.ds(lane * units, units)],
            )
            for lane in range(lanes)
        ]

    def wait(copies):
        for copy in copies:
            copy.wait()

    leaving = []
    for expert in range(count):
        arriving = [load(expert, 0)]
        if expert == 0:
            rows = {1: [start(inputs[1], blocks_ref.at[1])]}
        arriving.append(load(expert, 1))
        if expert == 0:
            slopes = {1: [start(inputs[3], grads_ref.at[1])]}
        arriving.append(load(expert, 2))
        if expert == 0:
            rows[0] = [start(inputs[0], blocks_ref.at[0])]
            slopes[0] = [start(inputs[2], grads_ref.at[0])]
        for side, out_ref in ((1, other_ref), (0, mine_ref)):
            block_ref, grad_ref = blocks_ref.at[side], grads_ref.at[side]
            if expert == 0:
                wait(rows[side])
            if side == 1:
                wait(arriving[0])
            number = expert_ref[expert]
            scale = gate_column(block_ref, width, number)
            block = block_ref[:, :width]
            gate = dot(block, held_ref[0], 1, 1)
            if side == 1:
                wait(arriving[1])
            up = dot(block, held_ref[1], 1, 1)
            if expert == 0:
                wait(slopes[side])
            if side == 1:
                wait(arriving[2])
            grad_raw = dot(grad_ref[...], held_ref[2], 1, 1)
            bent, slope = gelu_parts(gate)
            active = bent * up
            row_sum = jnp.sum(grad_raw * active, axis=1, keepdims=True)
            grad_active = grad_raw * scale
            grad_gate = (grad_active * up * slope).astype(BF)
            grad_up = (grad_active * bent).astype(BF)
            weighted = (active * scale).astype(BF)
            hidden_ref[side, 0] = grad_gate
            hidden_ref[side, 1] = grad_up
            hidden_ref[side, 2] = weighted
            term = dot(grad_gate, held_ref[0], 1, 0) + dot(grad_up, held_ref[1], 1, 0)
            hit = lax.broadcasted_iota(jnp.int32, (block.shape[0], 128), 1) == number
            gates = jnp.where(hit, row_sum, 0.0)
            ahead = dot(weighted, held_ref[2], 1, 0) if forward else None
            if count == 1:
                out_ref[:, :width] = term.astype(out_ref.dtype)
                out_ref[:, width:] = gates.astype(out_ref.dtype)
                if forward:
                    terms_refs[side][...] = ahead.astype(terms_refs[side].dtype)
            else:
                if expert > 0:
                    term = term + out_ref[:, :width].astype(F32)
                    gates = gates + out_ref[:, width:].astype(F32)
                out_ref[:, :width] = term.astype(out_ref.dtype)
                out_ref[:, width:] = gates.astype(out_ref.dtype)
                if forward:
                    if expert > 0:
                        ahead = ahead + terms_refs[side][...].astype(F32)
                    terms_refs[side][...] = ahead.astype(terms_refs[side].dtype)
            if expert == count - 1:
                leaving.append(start(out_ref, outs[side]))
                if forward:
                    leaving.append(start(terms_refs[side], outs[3 + side]))
        if expert > 0:
            wait(weights_leaving)
        weights_leaving = []
        for index in (2, 0, 1):
            total = None
            for side in (0, 1):
                right = grads_ref[side] if index == 2 else blocks_ref[side, :, :width]
                term = dot(hidden_ref[side, index], right, 0, 0)
                total = term if total is None else total + term
            weight_ref[index] = total.astype(BF)
            weights_leaving += [
                start(
                    weight_ref.at[index, pl.ds(lane * units, units)],
                    outs[2].at[lane, expert, index],
                )
                for lane in range(lanes)
            ]
    wait(leaving)
    wait(weights_leaving)


def row_parts(rows):
    parts = 1
    while rows % parts or rows // parts > ROWS_HELD:
        parts += 1
    return parts


def by_parts(call, *sides):
    rows = sides[0][0].shape[0]
    size = rows // row_parts(rows)
    return [
        call(*[[member[at : at + size] for member in side] for side in sides])
        for at in range(0, rows, size)
    ]


def experts_back(blocks, grads, weights, plan, forward):
    found = by_parts(
        lambda some, slopes: experts_back_part(some, slopes, weights, plan, forward), blocks, grads
    )
    if len(found) == 1:
        return found[0]
    found = list(zip(*found))
    return [
        sum(member.astype(F32) for member in members).astype(BF)
        if index == 2
        else jnp.concatenate(members, axis=0)
        for index, members in enumerate(found)
    ]


def experts_back_part(blocks, grads, weights, plan, forward, events=()):
    lanes, count, _, units, width = weights.shape
    rows = blocks[0].shape[0]
    hidden = lanes * units
    out_shape = [
        jax.ShapeDtypeStruct((rows, width + 128), BF),
        jax.ShapeDtypeStruct((rows, width + 128), BF),
        jax.ShapeDtypeStruct(weights.shape, BF),
    ]
    scratch = [
        pltpu.VMEM((2, rows, width + 128), BF),
        pltpu.VMEM((2, rows, width), BF),
        pltpu.VMEM((3, hidden, width), BF),
        pltpu.VMEM((rows, width + 128), BF),
        pltpu.VMEM((rows, width + 128), BF),
        pltpu.VMEM((2, 3, rows, hidden), BF),
        pltpu.VMEM((3, hidden, width), BF),
    ]
    if forward:
        for dtype in (BF, BF):
            out_shape.append(jax.ShapeDtypeStruct((rows, width), dtype))
            scratch.append(pltpu.VMEM((rows, width), dtype))
    scratch.append(pltpu.SemaphoreType.DMA((8 + 6 * lanes * count,)))
    anywhere = pl.BlockSpec(memory_space=pl.ANY)
    return pl.pallas_call(
        functools.partial(experts_back_kernel, forward, len(events)),
        in_specs=[pl.BlockSpec(memory_space=pltpu.SMEM)] + [anywhere] * (5 + len(events)),
        out_specs=[anywhere] * len(out_shape),
        out_shape=out_shape,
        scratch_shapes=scratch,
        compiler_params=kernel_params(0),
        name="experts_back",
    )(plan["experts"], *blocks, *grads, weights, *events)


def layer_backward(grad_out, grad_blocks, kept, weights, plan, forward, background):
    stream, attention_kept, middle, moe_in, blocks, chosen, within = kept
    mine, other, expert_grads, *terms = experts_back(
        blocks, grad_blocks, weights["experts"], plan, forward
    )
    events = background(mine)
    if events:
        other = tie(other, events[0], events[2])
    grad_moe = rows_reduce(mine, other, stream.shape[0])
    width = middle.shape[1]
    grad_gate = grad_moe[:, width : width + within.shape[1]] * within
    grad_moe = grad_moe[:, :width]
    gates = gate_values(dot(moe_in, weights["router"], 1, 0), chosen)
    grad_logits = gates * (grad_gate - jnp.sum(gates * grad_gate, axis=-1, keepdims=True))
    grad_logits = grad_logits.astype(BF)
    grad_moe = grad_moe + dot(grad_logits, weights["router"], 1, 1)
    grad_router = dot(moe_in, grad_logits, 0, 0)
    _, pull = jax.vjp(norm_rows, middle, weights["gains"][1])
    grad_middle, grad_gain_moe = pull(grad_moe)
    grad_middle = grad_middle + grad_out
    grad_stream, grad_q, grad_o, grad_kv, grad_gain = attention_backward(
        grad_middle, stream, attention_kept, weights, plan, events
    )
    extras = jnp.concatenate([grad_router, grad_gain[:, None], grad_gain_moe[:, None]], axis=1)
    grad_small = jnp.concatenate([grad_kv, pad_columns(extras)], axis=1)
    return grad_stream, (grad_q, grad_o, grad_small, expert_grads), terms


def pad_columns(values, columns=128):
    return jnp.pad(values, ((0, 0), (0, columns - values.shape[1])))


def holder():
    return (lax.axis_index("tensor") // 2) == lax.axis_index("section")


def head_columns(kv_weight, head):
    half = kv_weight.shape[1] // 2
    return jnp.concatenate(
        [kv_weight[:, head * HD : (head + 1) * HD], kv_weight[:, half + head * HD : half + (head + 1) * HD]],
        axis=1,
    )


def to_holders(own):
    lanes = lax.axis_size("tensor")
    pairs = [(t, lanes + t) for t in range(lanes // 2, lanes)]
    pairs += [(lanes + t, t) for t in range(lanes // 2)]
    moved = lax.ppermute(own, ("section", "tensor"), pairs)
    leading = lax.axis_index("section") == 0
    return jnp.where(leading, own, moved), jnp.where(leading, moved, own)


def from_holders(first, second):
    lanes = lax.axis_size("tensor")
    pairs = [(lanes + t, t) for t in range(lanes // 2, lanes)]
    pairs += [(t, lanes + t) for t in range(lanes // 2)]
    leading = lax.axis_index("section") == 0
    moved = lax.ppermute(jnp.where(leading, second, first), ("section", "tensor"), pairs)
    return jnp.where(holder(), jnp.where(leading, first, second), moved)


def reduce_small(parts, until=None):
    lanes = lax.axis_size("tensor")
    return lanes_reduce(parts.reshape(lanes, -1, parts.shape[1]), until)


def panels(grads):
    pieces = lax.axis_size("dp")
    return to_staged(grads.astype(BF).reshape(pieces, -1, grads.shape[1]))


def per_device(edge_in, routes, q_weight, o_weight, kv_weight, router, gains, w_in, w_out):
    section = lax.axis_index("section")
    leading = section == 0
    lanes = lax.axis_size("tensor")
    pieces = lax.axis_size("dp")
    rows = edge_in.shape[2]
    piece_rows = rows * lanes
    prompt_dev = PROMPT // pieces
    local, units, width = w_out.shape[1:]
    experts = local * pieces
    top = routes.shape[3]
    capacity = lanes * (
        (9 * piece_rows * top + 8 * experts * lanes - 1) // (8 * experts * lanes)
    )

    edge_kept = lax.dynamic_index_in_dim(edge_in[0], section, 0, keepdims=False)
    edge_got = section_swap(lax.dynamic_index_in_dim(edge_in[0], 1 - section, 0, keepdims=False))
    stream = jnp.where(leading, edge_kept, edge_got).astype(F32)
    cotangent = jnp.where(leading, edge_got, edge_kept)
    route_kept = lax.dynamic_index_in_dim(routes[0], section, 0, keepdims=False)
    route_got = section_swap(lax.dynamic_index_in_dim(routes[0], 1 - section, 0, keepdims=False))
    route_first = jnp.where(leading, route_kept, route_got)
    route_second = jnp.where(leading, route_got, route_kept)

    share = local // 2
    pack = jnp.stack([w_in[0, :, 0], w_in[0, :, 1], w_out[0]], axis=1)
    pack_kept = lax.dynamic_slice_in_dim(pack, section * share, share, 0)
    pack_got = section_swap(lax.dynamic_slice_in_dim(pack, (1 - section) * share, share, 0))
    pack_first = jnp.where(leading, pack_kept, pack_got)
    pack_second = jnp.where(leading, pack_got, pack_kept)
    experts_first = lax.all_gather(pack_first, "tensor", axis=0, tiled=False)

    masks = [route_masks(ids, experts, capacity) for ids in (route_first, route_second)]
    masks = [
        [
            lax.dynamic_slice_in_dim(member, lax.axis_index("tensor") * rows, rows, 0).astype(F32)
            for member in pair
        ]
        for pair in masks
    ]
    squares = to_holders(jnp.stack([q_weight[0], o_weight[0]]))
    extras = pad_columns(jnp.concatenate([router[0], gains[0].T], axis=1))
    heads = [jnp.concatenate([head_columns(kv_weight[0], h), extras], axis=1) for h in range(2)]
    small_kept = jnp.where(leading, heads[0], heads[1])
    small_got = section_swap(jnp.where(leading, heads[1], heads[0]))
    smalls = lanes_gather(
        jnp.concatenate(
            [jnp.where(leading, small_kept, small_got), jnp.where(leading, small_got, small_kept)],
            axis=1,
        ),
        0,
    )
    small_cols = small_kept.shape[1]
    query_cols = QH // 2 * HD
    panel = jnp.concatenate([holders_gather(squares[0][0]), smalls[:, :small_cols]], axis=1)
    qkv_first = from_staged(staged_gather(tie(panel, pack_first)))

    def layer_weights(layer, qkv):
        extras = qkv[:, query_cols + 2 * HD :]
        return {
            "qkv": qkv,
            "router": extras[:, :experts],
            "gains": extras[:, experts : experts + 2].T.astype(F32),
        }

    piece_index = lax.axis_index("dp")
    tables = rope_tables(own_places(rows, prompt_dev))
    plan = {
        "prompt_dev": prompt_dev,
        "rope": tables,
        "rope_both": [jnp.concatenate([table, table], axis=0) for table in tables],
        "bias": jnp.where(allowed_pairs(rows, piece_rows, prompt_dev), 0.0, NEGATIVE),
        "experts": piece_index * local + section * share + jnp.arange(share, dtype=jnp.int32),
    }
    def experts_rows(layer, middle, until=()):
        moe_in = norm_rows(middle, weights[layer]["gains"][1]).astype(BF)
        chosen, within = masks[layer]
        gates = gate_values(dot(moe_in, weights[layer]["router"], 1, 0), chosen) * within
        moe_rows = jnp.concatenate([moe_in, pad_columns(gates.astype(BF))], axis=1)
        return moe_in, rows_gather(moe_rows, until)

    weights = [layer_weights(0, qkv_first), None]
    weights[0]["experts"] = experts_first

    def fetch_first(normed, piece, prompt):
        o_first = holders_gather(tie(squares[0][1], panel), normed)
        return from_staged(staged_gather(o_first, (piece, prompt)))

    middle_first, attention_first = attention_forward(
        stream, weights[0], plan, (), fetch_first
    )
    prompt, attended = attention_first[2], attention_first[4]
    q_second = holders_gather(tie(squares[1][0], attended))
    moe_first, blocks_first = experts_rows(0, middle_first, (None, (experts_first, q_second)))
    mine, other = experts_forward(blocks_first, experts_first, plan)
    result = middle_first + rows_reduce(mine, other, rows)
    hidden = result.astype(BF).astype(F32)
    panel = jnp.concatenate([q_second, smalls[:, small_cols:]], axis=1)
    qkv_second = from_staged(staged_gather(panel, (other, result)))
    o_second = holders_gather(tie(squares[1][1], blocks_first[0]), result)

    grad_blocks = rows_gather(cotangent)
    weights[1] = layer_weights(1, qkv_second)
    weights[1]["experts"] = lax.all_gather(
        tie(pack_second, blocks_first[0]), "tensor", axis=0, tiled=False
    )

    def fetch_second(normed, piece, prompt):
        return from_staged(staged_gather(tie(o_second, normed), (piece, prompt)))

    middle_second, attention_second = attention_forward(
        hidden, weights[1], plan, (), fetch_second
    )
    moe_second, blocks_second = experts_rows(1, middle_second)

    kept = (hidden, attention_second, middle_second, moe_second, blocks_second, *masks[1])
    grad_stream, grads, terms = layer_backward(
        cotangent.astype(F32), grad_blocks, kept, weights[1], plan, True, lambda mine: ()
    )
    q_second, o_second, small_second, experts_second = grads
    half = q_second.shape[0]
    grad_out = grad_stream.astype(BF)
    grad_blocks = rows_gather(grad_out)
    second = []

    def beside_first(mine):
        squares = tie(jnp.concatenate([q_second, o_second], axis=0), grad_blocks[0])
        second.append(holders_reduce(squares, mine))
        second.append(reduce_stage(panels(small_second), dp_bits() - 1, mine))
        total = terms[0].astype(F32) + section_swap(terms[1]).astype(F32)
        total = tie(total, grad_blocks[0]).reshape(-1, rows, width)
        second.append(reduce_stage(total, dp_bits() - 1, mine))
        return second

    kept = (stream, attention_first, middle_first, moe_first, blocks_first, *masks[0])
    grad_stream, grads, _ = layer_backward(
        grad_out.astype(F32), grad_blocks, kept, weights[0], plan, False, beside_first
    )
    square_second, small_second, result = second
    small_second = reduce_rest(small_second)
    result = middle_second + reduce_rest(result)

    edge_kept = jnp.where(leading, grad_stream, result)
    edge_got = section_swap(jnp.where(leading, result, grad_stream))
    edge_out = jnp.where(
        leading, jnp.stack([edge_kept, edge_got]), jnp.stack([edge_got, edge_kept])
    )

    q_first, o_first, small_first, experts_first = grads
    square_first = holders_reduce(jnp.concatenate([q_first, o_first], axis=0))
    small_first = staged_reduce(panels(small_first))
    smalls = reduce_small(jnp.concatenate([small_first, small_second], axis=1))
    small_first, small_second = smalls[:, :small_cols], smalls[:, small_cols:]
    both = from_holders(square_first, square_second)
    grad_q, grad_o = both[:half], both[half:]
    small_kept = jnp.where(leading, small_first, small_second)
    small_got = section_swap(jnp.where(leading, small_second, small_first))
    key_values = jnp.where(
        leading,
        jnp.stack([small_kept[:, : 2 * HD], small_got[:, : 2 * HD]]),
        jnp.stack([small_got[:, : 2 * HD], small_kept[:, : 2 * HD]]),
    )
    grad_kv = jnp.concatenate(
        [key_values[0, :, :HD], key_values[1, :, :HD], key_values[0, :, HD:], key_values[1, :, HD:]],
        axis=1,
    )
    extras = small_kept[:, 2 * HD :] + small_got[:, 2 * HD :]

    summed = [
        lax.psum_scatter(member, "tensor", scatter_dimension=0, tiled=False)
        for member in (experts_first, experts_second)
    ]
    second_got = section_send(summed[1], 0)
    first_got = section_send(summed[0], 1)
    grad_experts = jnp.concatenate(
        [jnp.where(leading, summed[0], second_got), jnp.where(leading, first_got, summed[1])],
        axis=0,
    ).astype(F32)
    return (
        edge_out[None],
        grad_q[None],
        grad_o[None],
        grad_kv[None],
        extras[None, :, :experts],
        extras[:, experts : experts + 2].T[None],
        grad_experts[None, :, :2],
        grad_experts[None, :, 2],
    )


def solution(mesh):
    placed = (
        P("section", None, ("dp", "tensor"), None),
        P("section", None, "dp", None),
        P("section", "dp", "tensor"),
        P("section", "dp", "tensor"),
        P("section", ("dp", "tensor"), None),
        P("section", ("dp", "tensor"), None),
        P("section", None, ("dp", "tensor")),
        P("section", "dp", None, "tensor", None),
        P("section", "dp", "tensor", None),
    )
    return jax.shard_map(
        per_device,
        mesh=mesh,
        in_specs=placed,
        out_specs=(placed[0],) + placed[2:],
        check_vma=False,
    )
```
